128 devices in a mesh: rep: 4 (over y_hi, core), fsdp: 32 (over z, x, y_lo).
Axes of the slice: x: 4, y: 4 (y_hi: 2, y_lo: 2; y = y_hi * 2 + y_lo), z: 4, core: 2. Of those that a mesh axis runs over, the one named last changes fastest.
Arguments:
- activations: bfloat16 [2, 4, 12288, 8192], P(None, 'rep', 'fsdp'), may hold values from -6 to 6
- cotangent: bfloat16 [2, 4, 12288, 512], P(None, 'rep', 'fsdp'), may hold values from -6 to 6
- numerator: float32 [4, 8192, 512], P('rep', 'fsdp'), may hold values from -6 to 6
- weight: float32 [4], P('rep'), may hold values from 0.6 to 1.4
- inbox_num: float32 [4, 8192, 512], P('rep', 'fsdp'), may hold values from -3 to 3
- inbox_wt: float32 [4], P('rep'), may hold values from 0.3 to 0.7
- lengths: int32 [2, 4, 32], P(None, 'rep', 'fsdp'), may hold values from 96 to 384, as said below
- step_index: int32 [2], replicated, may hold values from 0 to 1023
Outputs:
- values: bfloat16 [2, 4, 12288, 512], P(None, 'rep', 'fsdp')
- numerator_out: float32 [4, 8192, 512], P('rep', 'fsdp')
- weight_out: float32 [4], P('rep')
- inbox_num_out: float32 [4, 8192, 512], P('rep', 'fsdp')
- inbox_wt_out: float32 [4], P('rep')
The draws below stay inside these ranges and needn't reach their ends.
Inputs may be any that keep to these rules, and one draw needn't show every extreme that they name: `lengths`: in each step some device's micro-batch has all 384 rows valid, and some other device's has 96.
All inputs are finite; a program needn't handle non-finite values.
Results may differ from the reference program's by a relative error of at most 0.02.
Values may be sent and summed in bfloat16 or wider, within the bound.
A program may use at most 192 MiB of HBM per device.

```python
import math
import jax
import jax.numpy as jnp
from jax import lax

D = 8192
HV = 512
TOK_DEV = 384
STEPS = 2
REPS = 4
SHARDS = 32
TOKENS = 12288


def draw_lengths(key, part):
    key = jax.random.fold_in(key, 11)
    first, second, third = jax.random.split(key, 3)
    total = REPS * SHARDS
    base = jax.random.randint(first, (STEPS, REPS, SHARDS), TOK_DEV // 4, TOK_DEV + 1)
    full_at = jax.random.randint(second, (STEPS, 1, 1), 0, total)
    short_at = (full_at + 1 + jax.random.randint(third, (STEPS, 1, 1), 0, total - 1)) % total
    places = jnp.arange(total, dtype=jnp.int32).reshape(1, REPS, SHARDS)
    result = jnp.where(places == short_at, TOK_DEV // 4, base)
    result = jnp.where(places == full_at, TOK_DEV, result)
    return result.astype(jnp.int32)


def strengthened(drawn, key, source, target, blocks, factor):
    owner, partner = [(jnp.arange(drawn.shape[dim]) // (drawn.shape[dim] // blocks)).reshape([-1 if axis == dim else 1 for axis in range(drawn.ndim)]) for dim in (source, target)]
    chosen = jax.random.permutation(key, blocks)[partner]
    strong = (owner == chosen) | (owner == (partner + blocks // 2) % blocks)
    return jnp.where(strong, factor * drawn, drawn)


def shard_levels(rng, shape, cuts, smallest, high):
    gain, own = 1.0, jax.random.fold_in(rng, 6)
    for dim, shards_of in cuts:
        draws = jnp.exp(jax.random.uniform(jax.random.fold_in(own, dim), (shards_of,), jnp.float32, smallest / len(cuts), high / len(cuts)))
        gain = gain * jnp.repeat(draws, shape[dim] // shards_of).reshape([-1 if axis == dim else 1 for axis in range(len(shape))])
    return gain


def gaussian(key, shape, width, bound, pieces=(), held_as=jnp.bfloat16):
    values = jax.random.normal(key, shape, jnp.float32) * width
    if len(pieces) > 0:
        values = shard_levels(key, shape, pieces, -0.22, 0.18) * values
    return jnp.clip(values, min=-bound, max=bound).astype(held_as)


def bell_draw_with(rng, extent, spread, limit, cuts, heavy, kind=jnp.bfloat16):
    values = spread * jax.random.normal(rng, extent, jnp.float32)
    if cuts:
        values = values * shard_levels(rng, extent, cuts, -0.22, 0.18)
    return jnp.clip(strengthened(values, jax.random.fold_in(rng, 3), *heavy), -limit, limit).astype(kind)


def setup_inputs(seed: int = 0) -> dict:
    splits = jax.random.split(jax.random.key(seed), 9)
    return {
        "activations": bell_draw_with(splits[0], (STEPS, REPS, TOKENS, D), 1.0, 6.0, ((1, 4), (2, 32)), (2, 3, 32, 2.75)),
        "cotangent": gaussian(splits[1], (STEPS, REPS, TOKENS, HV), 1.0, 6.0, ((1, 4), (2, 32))),
        "numerator": gaussian(splits[2], (REPS, D, HV), 1.0, 6.0, ((0, 4), (1, 32)), jnp.float32),
        "weight": jnp.clip(0.6 + 0.79999995 * jax.random.uniform(splits[3], (REPS,), jnp.float32) ** shard_levels(splits[3], (REPS,), ((0, 4),), -0.2, 0.2), 0.6, 1.4),
        "inbox_num": gaussian(splits[4], (REPS, D, HV), 0.5, 3.0, ((0, 4), (1, 32)), jnp.float32),
        "inbox_wt": jnp.clip(0.3 + 0.39999998 * jax.random.uniform(splits[5], (REPS,), jnp.float32) ** shard_levels(splits[5], (REPS,), ((0, 4),), -0.2, 0.2), 0.3, 0.7),
        "lengths": draw_lengths(jax.random.fold_in(splits[8], 71), 0),
        "step_index": jax.random.randint(splits[7], (STEPS,), 0, 1024).astype(jnp.int32),
    }


def reference(activations, cotangent, numerator, weight, inbox_num, inbox_wt, lengths, step_index):
    inv_root = 1.0 / math.sqrt(D)
    step_rate = 0.5 * math.sqrt(D / TOKENS)
    offset_bits = REPS.bit_length() - 1
    position = jnp.arange(TOKENS, dtype=jnp.int32) % TOK_DEV
    owner = jnp.arange(TOKENS, dtype=jnp.int32) // TOK_DEV
    outputs = []
    for section in range(STEPS):
        weights_bf = (numerator / weight[:, None, None]).astype(jnp.bfloat16)
        valid_mask = (position[None, :] < lengths[section][:, owner]).astype(jnp.float32)

        def forward(items):
            token_rows, weights_one, mask_one = items
            product = jnp.dot(token_rows, weights_one, preferred_element_type=jnp.float32)
            return (product * inv_root * mask_one[:, None]).astype(jnp.bfloat16)
        outputs.append(lax.map(forward, (activations[section], weights_bf, valid_mask)))
        upstream = (cotangent[section] * valid_mask[:, :, None]).astype(jnp.bfloat16)

        def gradient(items):
            token_rows, upstream_one = items
            token_blocks = token_rows.reshape(SHARDS, TOK_DEV, D)
            upstream_blocks = upstream_one.reshape(SHARDS, TOK_DEV, HV)

            def accumulate(running, block):
                partial_term = lax.dot_general(block[0], block[1], (((0,), (0,)), ((), ())), preferred_element_type=jnp.float32)
                rounded = lax.optimization_barrier(partial_term.astype(jnp.bfloat16))
                return (running + rounded.astype(jnp.float32), None)
            summed, unused = lax.scan(accumulate, jnp.zeros((D, HV), jnp.float32), (token_blocks, upstream_blocks))
            return summed * inv_root
        grads = lax.map(gradient, (activations[section], upstream))
        plan = 1.0 + 0.5 * jnp.cos(jnp.pi * step_index[section].astype(jnp.float32) / 1024.0)
        kept = 0.5 * (numerator - step_rate * plan * grads)
        kept_wt = 0.5 * weight
        shift_by = jnp.left_shift(jnp.int32(1), step_index[section] % offset_bits)
        numerator = kept + inbox_num
        weight = kept_wt + inbox_wt
        inbox_num = jnp.roll(kept, shift_by, axis=0)
        inbox_wt = jnp.roll(kept_wt, shift_by, axis=0)
    return (jnp.stack(outputs), numerator, weight, inbox_num, inbox_wt)
```

```python
import functools
import math

import jax
import jax.numpy as jnp
from jax import lax
from jax.experimental import pallas as pl
from jax.experimental.pallas import tpu as pltpu
from jax.sharding import PartitionSpec as P

MESH = pl.DeviceIdType.MESH
BF, F32 = jnp.bfloat16, jnp.float32
D, HV, TOK = 8192, 512, 384
INV_ROOT = 1.0 / math.sqrt(D)
HALF_TOK = TOK // 2
ROUTE = 64
HA = 160
SUB = 1024
ORDER = (
    "UPs.0", "AX.0", "T.0.0", "T.0.1", "T.0.2", "T.0.3", "T.0.4", "T.0.5", "T.0.6", "T.0.7", "UPs.1", "UT.0",
    "AY.0", "AZa.0", "C.0.0", "AZb.0", "AY1.0", "AYa.0", "AZe.0", "AZd.0", "D.0.0", "AZc.0", "C.0.1", "AYb.0",
    "AZg.0", "AZf.0", "D.0.1", "AYc.0", "C.0.2", "V.0.2", "V.0.1", "E.0.0", "T.1.0", "AZh.0", "D.0.2", "Fm.0",
    "T.1.1", "C.0.3", "AZi.0", "AYd.0", "V.0.3", "UT.1", "Fp.0", "E.0.1", "Gp.0", "T.1.2", "D.0.3", "V.0.0", "VR.0",
    "E.0.2", "Gm.0", "T.1.3", "C.1.0", "E.0.3", "T.1.4", "VM.0", "D.1.0", "H.0", "T.1.5", "C.1.1", "E.1.0", "J.0",
    "T.1.6", "D.1.1", "C.1.2", "I.0", "Fp.1", "T.1.7", "E.1.1", "Gp.1", "D.1.2", "Fm.1", "U.0", "AX.1", "E.1.2",
    "Gm.1", "C.1.3", "AY.1", "D.1.3", "H.1", "AY1.1", "AZa.1", "AZb.1", "AYa.1", "AZd.1", "V.1.3", "E.1.3", "J.1",
    "AZe.1", "AZf.1", "AZg.1", "I.1", "AZc.1", "AZh.1", "AYb.1", "U.1", "AZi.1", "V.1.2", "AYc.1", "V.1.1", "AYd.1",
    "V.1.0", "VR.1", "VM.1", "M",
)


def kernel(sc, length, act, cot, num, inbox, val, num_out, w_out, inbox_out, mw_out,
           ACT, Z, PT, PS, RSIB, RAH, RAF, RAY, RBY, RBH, RBF, RX, UPL, UP, UPT, VB, VR, VACC,
           ZS, KB, MSG, X1, WT, WR, ss, rs, credit):
    rep, fs = lax.axis_index("rep"), lax.axis_index("fsdp")
    yh, c = rep // 2, rep % 2
    z, x, yl = fs // 8, (fs // 2) % 4, fs % 2
    q = x % 2
    home = c == q
    guest = c != q
    my = 1 - yl

    def at(core, zz, xx, yy):
        return (yh * 2 + core, lax.rem(zz + 4, 4) * 8 + lax.rem(xx + 4, 4) * 2 + yy)

    sibling, mate = at(1 - c, z, x, yl), at(c, z, x, my)
    up_z, down_z = at(c, z + 1, x, yl), at(c, z + 3, x, yl)
    z0, zp, zm, z2 = z, lax.rem(z + 1, 4), lax.rem(z + 3, 4), lax.rem(z + 2, 4)
    chunk = (z2, zp, zm, z0)
    next1, next2 = (lax.rem(rep + 1, 4), fs), (lax.rem(rep + 2, 4), fs)

    names, pending = {}, {}

    def number(name):
        return names.setdefault(name, len(names))

    def remote(name, src, dst, to):
        k = number(name)
        r = number((name[0],) + name[2:]) if name[0].startswith("*") else k
        return pltpu.make_async_remote_copy(src, dst, ss.at[k], rs.at[r], device_id=to, device_id_type=MESH)

    def send(name, src, dst, to, guard=None):
        copy = remote(name, src, dst, to)
        pending[name] = (copy, guard)
        if guard is None:
            copy.start()
        else:
            pl.when(guard)(copy.start)

    def local(name, src, dst, guard):
        r = number((name[0],) + name[2:])
        pl.when(guard)(pltpu.make_async_copy(src, dst, rs.at[r]).start)

    def arrived(name, dst):
        r = number(name)
        pltpu.make_async_copy(dst, dst, rs.at[r]).wait()

    def sent(name):
        copy, guard = pending.pop(name)
        if guard is None:
            copy.wait_send()
        else:
            pl.when(guard)(copy.wait_send)

    def half(h):
        return pl.ds(pl.multiple_of(h * 128, 128), 128)

    rows_a = pl.ds(pl.multiple_of(c * 128, 64), ROUTE)
    rows_b = pl.ds(pl.multiple_of(c * 128 + ROUTE, 16), 128 - ROUTE)
    sib_a = pl.ds(pl.multiple_of((1 - c) * 128, 64), ROUTE)
    sib_b = pl.ds(pl.multiple_of((1 - c) * 128 + ROUTE, 16), 128 - ROUTE)
    hv_a, hv_b = pl.ds(0, HA), pl.ds(HA, 256 - HA)
    low, high, every = pl.ds(0, 2), pl.ds(2, 2), pl.ds(0, 4)

    def weight_at(s):
        return sc[4] if s == 0 else 0.5 * sc[4] + sc[5]

    def forward(name, s, zz, yy, mine):
        piece = Z.at[s, zz, :, yy, mine]
        send((name, s), piece, piece, sibling)

    def AX(s):
        block = num[0] if s == 0 else X1[...]
        ZS[s] = (block / weight_at(s)).astype(BF)

        def shard(h):
            return ZS.at[s, half(h)], Z.at[s, z, x, yl, half(h)]

        far = jnp.where(home, x + 2, x + 1)
        near = jnp.where(home, x, x + 3)
        send(("*AX", 0, s), *shard(0), at(0, z, far, yl))
        send(("*AX", 1, s), *shard(1), at(1, z, far, yl))
        send(("*AX", 2, s), *shard(1 - c), at(1 - c, z, near, yl))
        send(("*AX", 3, s), *shard(c), at(c, z, x + 3, yl), guest)
        local(("*AX", 4, s), *shard(c), home)

    def both_ways(plus, minus, s, piece):
        send((plus, s), piece, piece, up_z)
        send((minus, s), piece, piece, down_z)

    def AY(s):
        arrived(("*AX", s), Z.at[s, z, :, yl, half(c)])
        first, second = Z.at[s, z, :, yl, rows_a], Z.at[s, z, :, yl, rows_b]
        send(("YZy", s), first, first, mate)
        both_ways("ZYp", "ZYm", s, second)
        both_ways("YZop", "YZom", s, first)
        send(("ZYy0", s), second, second, mate)
        forward("S0", s, z, yl, half(c))

    def AY1(s):
        piece = Z.at[s, z, :, my, rows_a]
        arrived(("YZy", s), piece)
        both_ways("YZmp", "YZmm", s, piece)
        forward("S1", s, z, my, rows_a)

    def AZa(s):
        arrived(("ZYp", s), Z.at[s, zm, :, yl, rows_b])
        piece = Z.at[s, zm, low, yl, rows_b]
        send(("ZYfp", s), piece, piece, up_z)
        piece = Z.at[s, zm, :, yl, rows_b]
        send(("ZYym", s), piece, piece, mate)
        forward("Sa", s, zm, yl, rows_b)

    def AZb(s):
        arrived(("ZYm", s), Z.at[s, zp, :, yl, rows_b])
        piece = Z.at[s, zp, high, yl, rows_b]
        send(("ZYfm", s), piece, piece, down_z)
        piece = Z.at[s, zp, :, yl, rows_b]
        send(("ZYyp", s), piece, piece, mate)
        forward("Sb", s, zp, yl, rows_b)

    def AZc(s):
        arrived(("ZYfp", s), Z.at[s, z2, low, yl, rows_b])
        arrived(("ZYfm", s), Z.at[s, z2, high, yl, rows_b])
        piece = Z.at[s, z2, :, yl, rows_b]
        send(("ZYy2", s), piece, piece, mate)
        forward("Sc", s, z2, yl, rows_b)

    def AZd(s):
        piece = Z.at[s, zm, :, yl, rows_a]
        arrived(("YZop", s), piece)
        send(("YZfp", s), piece, piece, up_z)
        forward("Sd", s, zm, yl, rows_a)

    def AZe(s):
        arrived(("YZom", s), Z.at[s, zp, :, yl, rows_a])
        forward("Se", s, zp, yl, rows_a)

    def AZf(s):
        arrived(("YZmp", s), Z.at[s, zm, :, my, rows_a])
        forward("Sf", s, zm, my, rows_a)

    def AZg(s):
        piece = Z.at[s, zp, :, my, rows_a]
        arrived(("YZmm", s), piece)
        send(("YZfm", s), piece, piece, down_z)
        forward("Sg", s, zp, my, rows_a)

    def AZh(s):
        arrived(("YZfp", s), Z.at[s, z2, :, yl, rows_a])
        forward("Sh", s, z2, yl, rows_a)

    def AZi(s):
        arrived(("YZfm", s), Z.at[s, z2, :, my, rows_a])
        forward("Si", s, z2, my, rows_a)

    def AYany(source, name, zz):
        def run(s):
            arrived((source, s), Z.at[s, zz, :, my, rows_b])
            forward(name, s, zz, my, rows_b)
        return run

    def V(s, k):
        zz = chunk[k]
        if k == 3:
            arrived(("S0", s), Z.at[s, z, :, yl, half(1 - c)])
            arrived(("S1", s), Z.at[s, z, :, my, sib_a])
            arrived(("Sya", s), Z.at[s, z, :, my, sib_b])
        else:
            four = {2: ("Sa", "Sd", "Sf", "Syb"), 1: ("Sb", "Se", "Sg", "Syc"), 0: ("Sc", "Sh", "Si", "Syd")}[k]
            for name, yy, piece in zip(four, (yl, yl, my, my), (sib_b, sib_a, sib_a, sib_b)):
                arrived((name, s), Z.at[s, zz, :, yy, piece])

        def body(j, carry):
            columns = pl.ds(pl.multiple_of(zz * 2048 + j * 512, 512), 512)
            VACC[...] += jnp.dot(ACT[s, :, columns], Z[s, zz, j].reshape(512, HV), preferred_element_type=F32)
            return carry

        lax.fori_loop(0, 4, body, 0)

    def VC(s):
        VACC[...] = jnp.zeros_like(VACC)

    def VRet(s):
        VB[s] = (VACC[...] * INV_ROOT).astype(BF)
        top, low_rows = pl.ds(0, HALF_TOK), pl.ds(HALF_TOK, HALF_TOK)
        send(("*VR", 0, s), VB.at[s, top], VR.at[s, top], at(1 - c, z, x + 3, yl), guest)
        send(("*VR", 1, s), VB.at[s, low_rows], VR.at[s, low_rows], at(1 - c, z, x + 1, yl), guest)
        local(("*VR", 2, s), VB.at[s], VR.at[s], home)

    def valid(s):
        return lax.broadcasted_iota(jnp.int32, (TOK, HV), 0) < length[s]

    def VM(s):
        arrived(("*VR", s), VR.at[s])
        val[s, 0] = jnp.where(valid(s), VR[s].astype(F32), 0.0).astype(BF)

    def UPs(s):
        UPL[s] = jnp.where(valid(s), cot[s, 0].astype(F32), 0.0).astype(BF)
        top, low_rows = pl.ds(0, HALF_TOK), pl.ds(HALF_TOK, HALF_TOK)
        send(("*UP", 0, s), UPL.at[s, top], UP.at[s, top], at(1 - c, z, x + 1, yl), guest)
        send(("*UP", 1, s), UPL.at[s, low_rows], UP.at[s, low_rows], at(1 - c, z, x + 3, yl), guest)
        local(("*UP", 2, s), UPL.at[s], UP.at[s], home)

    def UT(s):
        arrived(("*UP", s), UP.at[s])
        mine = UP[s, :, pl.ds(pl.multiple_of(c * 256, 256), 256)]
        UPT[s, 0:256] = mine.astype(F32).T.astype(BF)
        other = UP[s, :, pl.ds(pl.multiple_of((1 - c) * 256, 256), 256)]
        UPT[s, 256:512] = other.astype(F32).T.astype(BF)

    def columns_of(k):
        return pl.ds(pl.multiple_of(chunk[k // 2] * 2048 + (k % 2) * SUB, SUB), SUB)

    def T(s, k):
        cols = columns_of(k)
        for j, to in ((0, x + 1), (1, x + 3)):
            rows = pl.ds(j * HALF_TOK, HALF_TOK)
            send(("*T", j, s, k), act.at[s, 0, rows, cols], ACT.at[s, rows, cols], at(1 - c, z, to, yl), guest)
        local(("*T", 2, s, k), act.at[s, 0, :, cols], ACT.at[s, :, cols], home)

    def C(s, k):
        zz = chunk[k]
        for j in (2 * k, 2 * k + 1):
            arrived(("*T", s, j), ACT.at[s, :, columns_of(j)])
        if s == 1:
            used = {0: ("Ahm", "Ahp", "Bhm", "Bhp"), 1: ("Afp", "Bfp"), 2: ("Afm", "Bfm"), 3: ("Ay",)}[k]
            for name in used:
                sent((name, 0))
            sent(("By", 0, k))
            sent(("SIB", 0, k))
            if k == 3:
                for part in range(2):
                    for j in range(4):
                        sent(("*X", j, part, 0))
            pl.semaphore_wait(credit.at[k], 1)

        def body(j, carry):
            cols = pl.ds(pl.multiple_of(zz * 2048 + j * 512, 512), 512)
            block = jnp.dot(UPT[s], ACT[s, :, cols], preferred_element_type=F32).astype(BF)
            for yy in range(2):
                PT[zz, j, yy] = block[0:256, yy * 256:(yy + 1) * 256]
                PS[zz, j, yy] = block[256:512, yy * 256:(yy + 1) * 256]
            return carry

        lax.fori_loop(0, 4, body, 0)
        send(("SIB", s, k), PS.at[zz], RSIB.at[zz], sibling)

    def add_into(count, target, *others):
        def body(j, carry):
            total = target(j)[...].astype(F32)
            for other in others:
                total = total + other(j)[...].astype(F32)
            target(j)[...] = total.astype(BF)
            return carry
        lax.fori_loop(0, count, body, 0)

    def Dd(s, k):
        zz = chunk[k]
        arrived(("SIB", s, k), RSIB.at[zz])
        add_into(8, lambda j: PT.at[zz, j // 2, j % 2], lambda j: RSIB.at[zz, j // 2, j % 2])
        if s == 0:
            pl.semaphore_signal(credit.at[k], inc=1, device_id=sibling, device_id_type=MESH)
        send(("By", s, k), PT.at[zz, :, my, hv_b], RBY.at[s, zz], mate)
        if k == 0:
            send(("Ahm", s), PT.at[zz, :, yl, hv_a], RAH.at[s, 0], down_z)
            send(("Ahp", s), PT.at[zz, :, my, hv_a], RAH.at[s, 1], up_z)

    def Ee(s, k):
        zz = chunk[k]
        arrived(("By", s, k), RBY.at[s, zz])
        add_into(4, lambda j: PT.at[zz, j, yl, hv_b], lambda j: RBY.at[s, zz, j])
        if k == 0:
            send(("Bhm", s), PT.at[zz, low, yl, hv_b], RBH.at[s, 0], down_z)
            send(("Bhp", s), PT.at[zz, high, yl, hv_b], RBH.at[s, 1], up_z)

    def Fm(s):
        arrived(("Ahm", s), RAH.at[s, 0])
        add_into(4, lambda j: PT.at[zm, j, yl, hv_a], lambda j: RAH.at[s, 0, j])
        send(("Afm", s), PT.at[zm, :, :, hv_a], RAF.at[s, 0], down_z)

    def Fp(s):
        arrived(("Ahp", s), RAH.at[s, 1])
        add_into(4, lambda j: PT.at[zp, j, my, hv_a], lambda j: RAH.at[s, 1, j])
        send(("Afp", s), PT.at[zp, :, :, hv_a], RAF.at[s, 1], up_z)

    def Gm(s):
        arrived(("Bhm", s), RBH.at[s, 0])
        add_into(2, lambda j: PT.at[zm, j, yl, hv_b], lambda j: RBH.at[s, 0, j])
        send(("Bfm", s), PT.at[zm, :, yl, hv_b], RBF.at[s, 0], down_z)

    def Gp(s):
        arrived(("Bhp", s), RBH.at[s, 1])
        add_into(2, lambda j: PT.at[zp, 2 + j, yl, hv_b], lambda j: RBH.at[s, 1, j])
        send(("Bfp", s), PT.at[zp, :, yl, hv_b], RBF.at[s, 1], up_z)

    def H(s):
        arrived(("Afm", s), RAF.at[s, 0])
        arrived(("Afp", s), RAF.at[s, 1])
        add_into(8, lambda j: PT.at[z, j // 2, j % 2, hv_a], lambda j: RAF.at[s, 0, j // 2, j % 2],
                 lambda j: RAF.at[s, 1, j // 2, j % 2])
        send(("Ay", s), PT.at[z, :, my, hv_a], RAY.at[s], mate)

    def owners(s, part, hv):
        def piece(xx, i):
            xx = lax.rem(xx, 4)
            return PT.at[z, xx, yl, hv], RX.at[s, i, c, hv]

        send(("*X", 0, part, s), *piece(x + 1, 1), at(q, z, x + 1, yl))
        send(("*X", 1, part, s), *piece(x + 3, 0), at(q, z, x + 3, yl))
        send(("*X", 2, part, s), *piece(x + 2, 1), at(q, z, x + 2, yl))
        send(("*X", 3, part, s), *piece(x, 0), sibling, guest)
        local(("*X", 4, part, s), *piece(x, 0), home)

    def I(s):
        arrived(("Ay", s), RAY.at[s])
        add_into(4, lambda j: PT.at[z, j, yl, hv_a], lambda j: RAY.at[s, j])
        owners(s, 0, hv_a)

    def J(s):
        arrived(("Bfm", s), RBF.at[s, 0])
        arrived(("Bfp", s), RBF.at[s, 1])
        add_into(4, lambda j: PT.at[z, j, yl, hv_b], lambda j: RBF.at[s, 0, j], lambda j: RBF.at[s, 1, j])
        owners(s, 1, hv_b)

    def chosen(s, which):
        return jnp.where(jnp.full((256, 256), sc[2 + s]) < 0.5, MSG[s, 0, :, which].astype(F32),
                         MSG[s, 1, :, which].astype(F32))

    def U(s):
        arrived(("*X", 0, s), RX.at[s, :, :, hv_a])
        arrived(("*X", 1, s), RX.at[s, :, :, hv_b])
        if s == 1:
            for j in range(2):
                arrived(("MSG", j, 0), MSG.at[0, j])
        for h in range(2):
            cols = slice(h * 256, (h + 1) * 256)
            grad = (RX[s, 0, h].astype(F32) + RX[s, 1, h].astype(F32)).T
            block = num[0, :, cols] if s == 0 else X1[:, cols]
            kept = 0.5 * (block - sc[s] * grad)
            KB[s, :, cols] = kept.astype(BF)
            if s == 0:
                X1[:, cols] = kept + inbox[0, :, cols]
            else:
                num_out[0, :, cols] = kept + chosen(0, cols)
        send(("MSG", 0, s), KB.at[s], MSG.at[s, 0], next1)
        send(("MSG", 1, s), KB.at[s], MSG.at[s, 1], next2)

    def M(s):
        for j in range(2):
            arrived(("WT", j), WR.at[j])
        even0, even1 = sc[2] < 0.5, sc[3] < 0.5
        w_out[0] = 0.5 * weight_at(1) + 0.5 * jnp.where(even0, WR[0, 0, 0], WR[1, 0, 0])
        mw_out[0] = 0.5 * (0.5 * jnp.where(even1, WR[0, 0, 0], WR[1, 0, 0])
                           + jnp.where(even1, WR[0, 4, 0], WR[1, 4, 0]))
        for j in range(2):
            arrived(("MSG", j, 1), MSG.at[1, j])
        for h in range(2):
            cols = slice(h * 256, (h + 1) * 256)
            inbox_out[0, :, cols] = chosen(1, cols)

    tasks = {
        "AX": AX, "AY": AY, "AY1": AY1, "AZa": AZa, "AZb": AZb, "AZc": AZc, "AZd": AZd, "AZe": AZe, "AZf": AZf,
        "AZg": AZg, "AZh": AZh, "AZi": AZi, "AYa": AYany("ZYy0", "Sya", z0), "AYb": AYany("ZYym", "Syb", zm),
        "AYc": AYany("ZYyp", "Syc", zp), "AYd": AYany("ZYy2", "Syd", z2), "V": V, "VR": VRet, "VM": VM,
        "UPs": UPs, "UT": UT, "T": T, "C": C, "D": Dd, "E": Ee, "Fm": Fm, "Fp": Fp, "Gm": Gm, "Gp": Gp,
        "H": H, "I": I, "J": J, "U": U,
    }

    barrier = pltpu.get_barrier_semaphore()
    others = [(lax.rem(rep + j, 4), fs) for j in (1, 2, 3)] + [mate, up_z, down_z]
    others += [at(core, z, x + j, yl) for core in (0, 1) for j in (1, 2, 3)]
    for other in others:
        pl.semaphore_signal(barrier, inc=1, device_id=other, device_id_type=MESH)
    pl.semaphore_wait(barrier, len(others))

    WT[...] = jnp.where(lax.broadcasted_iota(jnp.int32, (8, 128), 0) < 4, sc[4], sc[5])
    send(("WT", 0), WT, WR.at[0], next1)
    send(("WT", 1), WT, WR.at[1], next2)
    started = set()
    for entry in ORDER:
        name, *numbers = entry.split(".")
        if name == "M":
            M(0)
            continue
        if name == "V" and ("V", numbers[0]) not in started:
            started.add(("V", numbers[0]))
            VC(0)
        tasks[name](*map(int, numbers))
    for name in list(pending):
        sent(name)


def per_device(activations, cotangent, numerator, weight, inbox_num, inbox_wt, lengths, step_index):
    rate = 0.5 * math.sqrt(D / (TOK * 32)) * (1.0 + 0.5 * jnp.cos(jnp.pi * step_index.astype(F32) / 1024.0))
    scalars = jnp.concatenate([rate * INV_ROOT, (step_index % 2).astype(F32), weight, inbox_wt])
    length = lengths[:, 0, 0]
    vmem, smem, hbm = (pl.BlockSpec(memory_space=m) for m in (pltpu.VMEM, pltpu.SMEM, pl.ANY))
    hb = 256 - HA
    values, num_out, w_out, inbox_out, mw_out = pl.pallas_call(
        kernel,
        out_shape=(
            jax.ShapeDtypeStruct((2, 1, TOK, HV), BF),
            jax.ShapeDtypeStruct((1, 256, HV), F32),
            jax.ShapeDtypeStruct((1,), F32),
            jax.ShapeDtypeStruct((1, 256, HV), F32),
            jax.ShapeDtypeStruct((1,), F32),
        ),
        in_specs=[smem, smem, hbm, vmem, vmem, vmem],
        out_specs=(vmem, vmem, smem, vmem, smem),
        scratch_shapes=[
            pltpu.VMEM((2, TOK, D), BF),
            pltpu.VMEM((2, 4, 4, 2, 256, HV), BF),
            pltpu.VMEM((4, 4, 2, 256, 256), BF),
            pltpu.VMEM((4, 4, 2, 256, 256), BF),
            pltpu.VMEM((4, 4, 2, 256, 256), BF),
            pltpu.VMEM((2, 2, 4, HA, 256), BF),
            pltpu.VMEM((2, 2, 4, 2, HA, 256), BF),
            pltpu.VMEM((2, 4, HA, 256), BF),
            pltpu.VMEM((2, 4, 4, hb, 256), BF),
            pltpu.VMEM((2, 2, 2, hb, 256), BF),
            pltpu.VMEM((2, 2, 4, hb, 256), BF),
            pltpu.VMEM((2, 2, 2, 256, 256), BF),
            pltpu.VMEM((2, TOK, HV), BF),
            pltpu.VMEM((2, TOK, HV), BF),
            pltpu.VMEM((2, HV, TOK), BF),
            pltpu.VMEM((2, TOK, HV), BF),
            pltpu.VMEM((2, TOK, HV), BF),
            pltpu.VMEM((TOK, HV), F32),
            pltpu.VMEM((2, 256, HV), BF),
            pltpu.VMEM((2, 256, HV), BF),
            pltpu.VMEM((2, 2, 256, HV), BF),
            pltpu.VMEM((256, HV), F32),
            pltpu.VMEM((8, 128), F32),
            pltpu.VMEM((2, 8, 128), F32),
            pltpu.SemaphoreType.DMA((256,)),
            pltpu.SemaphoreType.DMA((256,)),
            pltpu.SemaphoreType.REGULAR((4,)),
        ],
        compiler_params=pltpu.CompilerParams(
            collective_id=0, has_side_effects=True, vmem_limit_bytes=63 * 2**20
        ),
        cost_estimate=pl.CostEstimate(flops=4 * 2 * TOK * D * HV, bytes_accessed=2 * TOK * D * 2, transcendentals=0),
        name="push_steps",
    )(scalars, length, activations, cotangent, numerator, inbox_num)
    return values, num_out, w_out, inbox_out, mw_out


def solution(mesh):
    in_specs = (
        P(None, "rep", "fsdp", None),
        P(None, "rep", "fsdp", None),
        P("rep", "fsdp", None),
        P("rep"),
        P("rep", "fsdp", None),
        P("rep"),
        P(None, "rep", "fsdp"),
        P(),
    )
    out_specs = (
        P(None, "rep", "fsdp", None),
        P("rep", "fsdp", None),
        P("rep"),
        P("rep", "fsdp", None),
        P("rep"),
    )
    return jax.shard_map(
        per_device, mesh=mesh, in_specs=in_specs, out_specs=out_specs, check_vma=False
    )
```

```python
import functools
import math

import jax
import jax.numpy as jnp
from jax import lax
from jax.experimental import pallas as pl
from jax.experimental.pallas import tpu as pltpu
from jax.sharding import PartitionSpec as P

MESH = pl.DeviceIdType.MESH
BF, F32 = jnp.bfloat16, jnp.float32
D, HV, TOK = 8192, 512, 384
INV_ROOT = 1.0 / math.sqrt(D)
HALF_TOK = TOK // 2
ROUTE = 80
HA = 160
SUB = 1024
ORDER = (
    "UPs.0", "AX.0", "T.0.0", "UT.0", "T.0.1", "AY.0", "AYz.0", "T.0.2", "AYo.0", "T.0.3", "C.0.0", "UPs.1",
    "T.0.4", "AZa.0", "AZb.0", "AY1.0", "AYn.0", "C.0.1", "T.0.5", "T.0.6", "FS1.0", "C.0.2", "D.0.0", "AH.0",
    "UT.1", "C.0.3", "AZc.0", "C.0.4", "FSf.0", "T.0.7", "D.0.1", "T.1.0", "AZby.0", "T.1.1", "AZd.0", "AZg.0",
    "E.0.0", "C.0.5", "FSyd.0", "D.0.2", "FS0.0", "FSc.0", "C.0.6", "AZay.0", "FSya.0", "C.0.7", "E.0.1", "Fmm.0",
    "Fpm.0", "T.1.2", "D.0.3", "Fpo.0", "E.0.2", "C.1.0", "Fmo.0", "T.1.3", "C.1.1", "T.1.4", "Gml.0", "Gpl.0",
    "Hm.0", "T.1.5", "D.1.0", "Gph.0", "Gmh.0", "FSyb.0", "C.1.2", "C.1.3", "AH.1", "E.0.3", "C.1.4", "FSyc.0",
    "FSe.0", "Ho.0", "I.0", "D.1.1", "C.1.5", "FSa.0", "Fpo.1", "J.0", "FSd.0", "E.1.0", "T.1.6", "D.1.2", "Fmm.1",
    "Fmo.1", "U.0", "AX.1", "T.1.7", "Fpm.1", "MS.0", "C.1.6", "AY.1", "FSi.0", "FSh.0", "FSg.0", "AYn.1", "AYz.1",
    "C.1.7", "E.1.1", "AYo.1", "FSb.0", "AZa.1", "FSa.1", "V.0.0", "D.1.3", "E.1.2", "AY1.1", "AZb.1", "V.0.2",
    "Hm.1", "Gph.1", "AZay.1", "FSya.1", "V.0.3", "AZby.1", "Gpl.1", "V.0.1", "Gmh.1", "FS0.1", "AZd.1", "Gml.1",
    "FSf.1", "VR.0", "AZg.1", "FS1.1", "FSe.1", "AZc.1", "Ho.1", "FSd.1", "I.1", "E.1.3", "FSyb.1", "FSg.1", "VM.0",
    "FSc.1", "J.1", "V.1.3", "FSb.1", "V.1.2", "FSyc.1", "FSh.1", "U.1", "MS.1", "FSi.1", "FSyd.1", "V.1.1",
    "V.1.0", "VR.1", "VM.1", "M",
)


def kernel(index, length, weight, inbox_wt, act, cot, num, inbox, val, num_out, w_out, inbox_out, mw_out,
           ACT, Z, PT, PS, RSIB, RAH, RAF, RAY, RBY, RBH, RBF, RX, UPL, UP, UPT, VB, VR, VACC,
           ZS, KB, MSG, X1, WT, WR, COT, NUM, INB, RATE, ss, rs, io, credit):
    rep, fs = lax.axis_index("rep"), lax.axis_index("fsdp")
    yh, c = rep // 2, rep % 2
    z, x, yl = fs // 8, (fs // 2) % 4, fs % 2
    q = x % 2
    home = c == q
    guest = c != q
    my = 1 - yl

    def at(core, zz, xx, yy):
        return (yh * 2 + core, lax.rem(zz + 4, 4) * 8 + lax.rem(xx + 4, 4) * 2 + yy)

    sibling, mate = at(1 - c, z, x, yl), at(c, z, x, my)
    up_z, down_z = at(c, z + 1, x, yl), at(c, z + 3, x, yl)
    z0, zp, zm, z2 = z, lax.rem(z + 1, 4), lax.rem(z + 3, 4), lax.rem(z + 2, 4)
    chunk = (z2, zp, zm, z0)
    next1, next2 = (lax.rem(rep + 1, 4), fs), (lax.rem(rep + 2, 4), fs)

    inputs = [pltpu.make_async_copy(*pair, io.at[i])
              for i, pair in enumerate([(num.at[0], NUM), (cot.at[:, 0], COT), (inbox.at[0], INB)])]
    for copy in inputs:
        copy.start()
    names, pending = {}, {}

    def number(name):
        return names.setdefault(name, len(names))

    def remote(name, src, dst, to):
        k = number(name)
        r = number((name[0],) + name[2:]) if name[0].startswith("*") else k
        return pltpu.make_async_remote_copy(src, dst, ss.at[k], rs.at[r], device_id=to, device_id_type=MESH)

    def send(name, src, dst, to, guard=None):
        copy = remote(name, src, dst, to)
        pending[name] = (copy, guard)
        if guard is None:
            copy.start()
        else:
            pl.when(guard)(copy.start)

    def local(name, src, dst, guard):
        r = number((name[0],) + name[2:])
        pl.when(guard)(pltpu.make_async_copy(src, dst, rs.at[r]).start)

    def arrived(name, dst):
        r = number(name)
        pltpu.make_async_copy(dst, dst, rs.at[r]).wait()

    def sent(name):
        copy, guard = pending.pop(name)
        if guard is None:
            copy.wait_send()
        else:
            pl.when(guard)(copy.wait_send)

    def half(h):
        return pl.ds(pl.multiple_of(h * 128, 128), 128)

    rows_a = pl.ds(pl.multiple_of(c * 128, 64), ROUTE)
    rows_b = pl.ds(pl.multiple_of(c * 128 + ROUTE, 16), 128 - ROUTE)
    sib_a = pl.ds(pl.multiple_of((1 - c) * 128, 64), ROUTE)
    sib_b = pl.ds(pl.multiple_of((1 - c) * 128 + ROUTE, 16), 128 - ROUTE)
    hv_a, hv_b = pl.ds(0, HA), pl.ds(HA, 256 - HA)
    low, high, every = pl.ds(0, 2), pl.ds(2, 2), pl.ds(0, 4)

    def weight_at(s):
        return weight[0] if s == 0 else 0.5 * weight[0] + inbox_wt[0]

    def forward(name, s, zz, yy, mine):
        piece = Z.at[s, zz, :, yy, mine]
        send((name, s), piece, piece, sibling)

    def AX(s):
        if s == 0:
            inputs[0].wait()
        block = NUM[...] if s == 0 else X1[...]
        ZS[s] = (block / weight_at(s)).astype(BF)

        def shard(h):
            return ZS.at[s, half(h)], Z.at[s, z, x, yl, half(h)]

        far = jnp.where(home, x + 2, x + 1)
        near = jnp.where(home, x, x + 3)
        send(("*AX", 0, s), *shard(0), at(0, z, far, yl))
        send(("*AX", 1, s), *shard(1), at(1, z, far, yl))
        send(("*AX", 2, s), *shard(1 - c), at(1 - c, z, near, yl))
        send(("*AX", 3, s), *shard(c), at(c, z, x + 3, yl), guest)
        local(("*AX", 4, s), *shard(c), home)

    def both_ways(plus, minus, s, piece):
        send((plus, s), piece, piece, up_z)
        send((minus, s), piece, piece, down_z)

    def gathered(s, zz, yy, rows, part=every):
        return Z.at[s, zz, part, yy, rows]

    def pass_on(name, to, zz, yy, rows, source=None, part=every):
        def run(s):
            piece = gathered(s, zz, yy, rows, part)
            if source is not None:
                arrived((source, s), piece)
            send((name, s), piece, piece, to)
        return run

    def AY(s):
        arrived(("*AX", s), gathered(s, z, yl, half(c)))
        pass_on("YZy", mate, z, yl, rows_a)(s)

    def AYz(s):
        pass_on("ZYp", up_z, z, yl, rows_b)(s)
        pass_on("ZYm", down_z, z, yl, rows_b)(s)

    def AYo(s):
        pass_on("YZop", up_z, z, yl, rows_a)(s)
        pass_on("YZom", down_z, z, yl, rows_a)(s)

    def AY1(s):
        pass_on("YZmp", up_z, z, my, rows_a, "YZy")(s)
        pass_on("YZmm", down_z, z, my, rows_a)(s)

    def AZa(s):
        arrived(("ZYp", s), gathered(s, zm, yl, rows_b))
        pass_on("ZYfp", up_z, zm, yl, rows_b, None, low)(s)

    def AZb(s):
        arrived(("ZYm", s), gathered(s, zp, yl, rows_b))
        pass_on("ZYfm", down_z, zp, yl, rows_b, None, high)(s)

    def AZc(s):
        arrived(("ZYfp", s), gathered(s, z2, yl, rows_b, low))
        arrived(("ZYfm", s), gathered(s, z2, yl, rows_b, high))
        pass_on("ZYy2", mate, z2, yl, rows_b)(s)

    def V(s, k):
        zz = chunk[k]
        if k == 3:
            arrived(("S0", s), Z.at[s, z, :, yl, half(1 - c)])
            arrived(("S1", s), Z.at[s, z, :, my, sib_a])
            arrived(("Sya", s), Z.at[s, z, :, my, sib_b])
        else:
            four = {2: ("Sa", "Sd", "Sf", "Syb"), 1: ("Sb", "Se", "Sg", "Syc"), 0: ("Sc", "Sh", "Si", "Syd")}[k]
            for name, yy, piece in zip(four, (yl, yl, my, my), (sib_b, sib_a, sib_a, sib_b)):
                arrived((name, s), Z.at[s, zz, :, yy, piece])

        def body(j, carry):
            columns = pl.ds(pl.multiple_of(zz * 2048 + j * 512, 512), 512)
            VACC[...] += jnp.dot(ACT[s, :, columns], Z[s, zz, j].reshape(512, HV), preferred_element_type=F32)
            return carry

        lax.fori_loop(0, 4, body, 0)

    def VC(s):
        VACC[...] = jnp.zeros_like(VACC)

    def VRet(s):
        VB[s] = (VACC[...] * INV_ROOT).astype(BF)
        top, low_rows = pl.ds(0, HALF_TOK), pl.ds(HALF_TOK, HALF_TOK)
        send(("*VR", 0, s), VB.at[s, top], VR.at[s, top], at(1 - c, z, x + 3, yl), guest)
        send(("*VR", 1, s), VB.at[s, low_rows], VR.at[s, low_rows], at(1 - c, z, x + 1, yl), guest)
        local(("*VR", 2, s), VB.at[s], VR.at[s], home)

    def valid(s):
        return lax.broadcasted_iota(jnp.int32, (TOK, HV), 0) < length[s]

    def VM(s):
        arrived(("*VR", s), VR.at[s])
        VR[s] = jnp.where(valid(s), VR[s].astype(F32), 0.0).astype(BF)
        result(VR.at[s], val.at[s, 0])

    outputs = []

    def result(src, dst):
        outputs.append(pltpu.make_async_copy(src, dst, io.at[3 + len(outputs)]))
        outputs[-1].start()

    def UPs(s):
        if s == 0:
            inputs[1].wait()
        UPL[s] = jnp.where(valid(s), COT[s].astype(F32), 0.0).astype(BF)
        top, low_rows = pl.ds(0, HALF_TOK), pl.ds(HALF_TOK, HALF_TOK)
        send(("*UP", 0, s), UPL.at[s, top], UP.at[s, top], at(1 - c, z, x + 1, yl), guest)
        send(("*UP", 1, s), UPL.at[s, low_rows], UP.at[s, low_rows], at(1 - c, z, x + 3, yl), guest)
        local(("*UP", 2, s), UPL.at[s], UP.at[s], home)

    def UT(s):
        arrived(("*UP", s), UP.at[s])
        mine = UP[s, :, pl.ds(pl.multiple_of(c * 256, 256), 256)]
        UPT[s, 0:256] = mine.astype(F32).T.astype(BF)
        other = UP[s, :, pl.ds(pl.multiple_of((1 - c) * 256, 256), 256)]
        UPT[s, 256:512] = other.astype(F32).T.astype(BF)

    def columns_of(k):
        return pl.ds(pl.multiple_of(chunk[k // 2] * 2048 + (k % 2) * SUB, SUB), SUB)

    def T(s, k):
        cols = columns_of(k)
        for j, to in ((0, x + 1), (1, x + 3)):
            rows = pl.ds(j * HALF_TOK, HALF_TOK)
            send(("*T", j, s, k), act.at[s, 0, rows, cols], ACT.at[s, rows, cols], at(1 - c, z, to, yl), guest)
        local(("*T", 2, s, k), act.at[s, 0, :, cols], ACT.at[s, :, cols], home)

    def C(s, k):
        zz = chunk[k // 2]
        arrived(("*T", s, k), ACT.at[s, :, columns_of(k)])
        if s == 1 and k % 2 == 0:
            used = {0: ("Ahm", "Ahp", "Bhm", "Bhp"), 1: ("Afpo", "Afpm", "Bfpl", "Bfph"),
                    2: ("Afmo", "Afmm", "Bfml", "Bfmh"), 3: ("Ay",)}[k // 2]
            for name in used:
                sent((name, 0))
            sent(("By", 0, k // 2))
            sent(("SIB", 0, k))
            sent(("SIB", 0, k + 1))
            if k == 6:
                for part in range(2):
                    for j in range(4):
                        sent(("*X", j, part, 0))
            pl.semaphore_wait(credit.at[k // 2], 1)

        def body(j, carry):
            cols = pl.ds(pl.multiple_of(zz * 2048 + j * 512, 512), 512)
            block = jnp.dot(UPT[s], ACT[s, :, cols], preferred_element_type=F32).astype(BF)
            for yy in range(2):
                PT[zz, j, yy] = block[0:256, yy * 256:(yy + 1) * 256]
                PS[zz, j, yy] = block[256:512, yy * 256:(yy + 1) * 256]
            return carry

        first = 2 * (k % 2)
        lax.fori_loop(first, first + 2, body, 0)
        pair = pl.ds(first, 2)
        send(("SIB", s, k), PS.at[zz, pair], RSIB.at[zz, pair], sibling)

    def add_into(count, target, *others):
        def body(j, carry):
            total = target(j)[...].astype(F32)
            for other in others:
                total = total + other(j)[...].astype(F32)
            target(j)[...] = total.astype(BF)
            return carry
        lax.fori_loop(0, count, body, 0)

    def Dd(s, k):
        zz = chunk[k]
        arrived(("SIB", s, 2 * k), RSIB.at[zz, low])
        arrived(("SIB", s, 2 * k + 1), RSIB.at[zz, high])
        add_into(8, lambda j: PT.at[zz, j // 2, j % 2], lambda j: RSIB.at[zz, j // 2, j % 2])
        if s == 0:
            pl.semaphore_signal(credit.at[k], inc=1, device_id=sibling, device_id_type=MESH)
        send(("By", s, k), PT.at[zz, :, my, hv_b], RBY.at[s, zz], mate)

    def AH(s):
        send(("Ahm", s), PT.at[z2, :, yl, hv_a], RAH.at[s, 0], down_z)
        send(("Ahp", s), PT.at[z2, :, my, hv_a], RAH.at[s, 1], up_z)

    def Ee(s, k):
        zz = chunk[k]
        arrived(("By", s, k), RBY.at[s, zz])
        add_into(4, lambda j: PT.at[zz, j, yl, hv_b], lambda j: RBY.at[s, zz, j])
        if k == 0:
            send(("Bhm", s), PT.at[zz, low, yl, hv_b], RBH.at[s, 0], down_z)
            send(("Bhp", s), PT.at[zz, high, yl, hv_b], RBH.at[s, 1], up_z)

    def Fmm(s):
        send(("Afmm", s), PT.at[zm, :, my, hv_a], RAF.at[s, 0, :, my], down_z)

    def Fmo(s):
        arrived(("Ahm", s), RAH.at[s, 0])
        add_into(4, lambda j: PT.at[zm, j, yl, hv_a], lambda j: RAH.at[s, 0, j])
        send(("Afmo", s), PT.at[zm, :, yl, hv_a], RAF.at[s, 0, :, yl], down_z)

    def Fpo(s):
        send(("Afpo", s), PT.at[zp, :, yl, hv_a], RAF.at[s, 1, :, yl], up_z)

    def Fpm(s):
        arrived(("Ahp", s), RAH.at[s, 1])
        add_into(4, lambda j: PT.at[zp, j, my, hv_a], lambda j: RAH.at[s, 1, j])
        send(("Afpm", s), PT.at[zp, :, my, hv_a], RAF.at[s, 1, :, my], up_z)

    def Gmh(s):
        send(("Bfmh", s), PT.at[zm, high, yl, hv_b], RBF.at[s, 0, high], down_z)

    def Gml(s):
        arrived(("Bhm", s), RBH.at[s, 0])
        add_into(2, lambda j: PT.at[zm, j, yl, hv_b], lambda j: RBH.at[s, 0, j])
        send(("Bfml", s), PT.at[zm, low, yl, hv_b], RBF.at[s, 0, low], down_z)

    def Gpl(s):
        send(("Bfpl", s), PT.at[zp, low, yl, hv_b], RBF.at[s, 1, low], up_z)

    def Gph(s):
        arrived(("Bhp", s), RBH.at[s, 1])
        add_into(2, lambda j: PT.at[zp, 2 + j, yl, hv_b], lambda j: RBH.at[s, 1, j])
        send(("Bfph", s), PT.at[zp, high, yl, hv_b], RBF.at[s, 1, high], up_z)

    def H(s, yy, minus, plus):
        arrived((minus, s), RAF.at[s, 0, :, yy])
        arrived((plus, s), RAF.at[s, 1, :, yy])
        add_into(4, lambda j: PT.at[z, j, yy, hv_a], lambda j: RAF.at[s, 0, j, yy], lambda j: RAF.at[s, 1, j, yy])

    def Hm(s):
        H(s, my, "Afmm", "Afpm")
        send(("Ay", s), PT.at[z, :, my, hv_a], RAY.at[s], mate)

    def Ho(s):
        H(s, yl, "Afmo", "Afpo")

    def owners(s, part, hv):
        def piece(xx, i):
            xx = lax.rem(xx, 4)
            return PT.at[z, xx, yl, hv], RX.at[s, i, c, hv]

        send(("*X", 0, part, s), *piece(x + 1, 1), at(q, z, x + 1, yl))
        send(("*X", 1, part, s), *piece(x + 3, 0), at(q, z, x + 3, yl))
        send(("*X", 2, part, s), *piece(x + 2, 1), at(q, z, x + 2, yl))
        send(("*X", 3, part, s), *piece(x, 0), sibling, guest)
        local(("*X", 4, part, s), *piece(x, 0), home)

    def I(s):
        arrived(("Ay", s), RAY.at[s])
        add_into(4, lambda j: PT.at[z, j, yl, hv_a], lambda j: RAY.at[s, j])
        owners(s, 0, hv_a)

    def J(s):
        for name, way, part in (("Bfml", 0, low), ("Bfmh", 0, high), ("Bfpl", 1, low), ("Bfph", 1, high)):
            arrived((name, s), RBF.at[s, way, part])
        add_into(4, lambda j: PT.at[z, j, yl, hv_b], lambda j: RBF.at[s, 0, j], lambda j: RBF.at[s, 1, j])
        owners(s, 1, hv_b)

    def chosen(s, which):
        return jnp.where(jnp.full((256, 256), index[s] % 2) == 0, MSG[s, 0, :, which].astype(F32),
                         MSG[s, 1, :, which].astype(F32))

    def U(s):
        arrived(("*X", 0, s), RX.at[s, :, :, hv_a])
        arrived(("*X", 1, s), RX.at[s, :, :, hv_b])
        if s == 0:
            inputs[2].wait()
            for j in range(2):
                step = jnp.full((8, 128), index[j]).astype(F32)
                RATE[j] = 0.5 * math.sqrt(D / (TOK * 32)) * INV_ROOT * (1.0 + 0.5 * jnp.cos(jnp.pi * step / 1024.0))
        if s == 1:
            for j in range(2):
                arrived(("MSG", j, 0), MSG.at[0, j])
        for h in range(2):
            cols = slice(h * 256, (h + 1) * 256)
            grad = (RX[s, 0, h].astype(F32) + RX[s, 1, h].astype(F32)).T
            block = NUM[:, cols] if s == 0 else X1[:, cols]
            kept = 0.5 * (block - RATE[s, 0:1, 0:1] * grad)
            KB[s, :, cols] = kept.astype(BF)
            if s == 0:
                X1[:, cols] = kept + INB[:, cols]
            else:
                X1[:, cols] = kept + chosen(0, cols)
        if s == 1:
            result(X1, num_out.at[0])

    def MS(s):
        send(("MSG", 0, s), KB.at[s], MSG.at[s, 0], next1)
        send(("MSG", 1, s), KB.at[s], MSG.at[s, 1], next2)

    def M(s):
        for j in range(2):
            arrived(("WT", j), WR.at[j])
        even0, even1 = index[0] % 2 == 0, index[1] % 2 == 0
        w_out[0] = 0.5 * weight_at(1) + 0.5 * jnp.where(even0, WR[0, 0, 0], WR[1, 0, 0])
        mw_out[0] = 0.5 * (0.5 * jnp.where(even1, WR[0, 0, 0], WR[1, 0, 0])
                           + jnp.where(even1, WR[0, 4, 0], WR[1, 4, 0]))
        for j in range(2):
            arrived(("MSG", j, 1), MSG.at[1, j])
        for h in range(2):
            cols = slice(h * 256, (h + 1) * 256)
            INB[:, cols] = chosen(1, cols)
        result(INB, inbox_out.at[0])

    tasks = {
        "AX": AX, "AY": AY, "AYz": AYz, "AYo": AYo, "AYn": pass_on("ZYy0", mate, z, yl, rows_b), "AY1": AY1,
        "AZa": AZa, "AZb": AZb, "AZc": AZc,
        "AZay": pass_on("ZYym", mate, zm, yl, rows_b), "AZby": pass_on("ZYyp", mate, zp, yl, rows_b),
        "AZd": pass_on("YZfp", up_z, zm, yl, rows_a, "YZop"), "AZg": pass_on("YZfm", down_z, zp, my, rows_a, "YZmm"),
        "FS0": pass_on("S0", sibling, z, yl, half(c)), "FS1": pass_on("S1", sibling, z, my, rows_a),
        "FSa": pass_on("Sa", sibling, zm, yl, rows_b), "FSb": pass_on("Sb", sibling, zp, yl, rows_b),
        "FSc": pass_on("Sc", sibling, z2, yl, rows_b), "FSd": pass_on("Sd", sibling, zm, yl, rows_a),
        "FSe": pass_on("Se", sibling, zp, yl, rows_a, "YZom"), "FSf": pass_on("Sf", sibling, zm, my, rows_a, "YZmp"),
        "FSg": pass_on("Sg", sibling, zp, my, rows_a), "FSh": pass_on("Sh", sibling, z2, yl, rows_a, "YZfp"),
        "FSi": pass_on("Si", sibling, z2, my, rows_a, "YZfm"),
        "FSya": pass_on("Sya", sibling, z0, my, rows_b, "ZYy0"), "FSyb": pass_on("Syb", sibling, zm, my, rows_b, "ZYym"),
        "FSyc": pass_on("Syc", sibling, zp, my, rows_b, "ZYyp"), "FSyd": pass_on("Syd", sibling, z2, my, rows_b, "ZYy2"),
        "V": V, "VR": VRet, "VM": VM, "UPs": UPs, "UT": UT, "T": T, "C": C, "D": Dd, "E": Ee, "AH": AH,
        "Fmm": Fmm, "Fmo": Fmo, "Fpo": Fpo, "Fpm": Fpm, "Gmh": Gmh, "Gml": Gml, "Gpl": Gpl, "Gph": Gph,
        "Hm": Hm, "Ho": Ho, "I": I, "J": J, "U": U, "MS": MS,
    }

    barrier = pltpu.get_barrier_semaphore()
    others = [(lax.rem(rep + j, 4), fs) for j in (1, 2, 3)] + [mate, up_z, down_z]
    others += [at(core, z, x + j, yl) for core in (0, 1) for j in (1, 2, 3)]
    for other in others:
        pl.semaphore_signal(barrier, inc=1, device_id=other, device_id_type=MESH)
    pl.semaphore_wait(barrier, len(others))

    WT[...] = jnp.where(lax.broadcasted_iota(jnp.int32, (8, 128), 0) < 4, weight[0], inbox_wt[0])
    send(("WT", 0), WT, WR.at[0], next1)
    send(("WT", 1), WT, WR.at[1], next2)
    started = set()
    for entry in ORDER:
        name, *numbers = entry.split(".")
        if name == "M":
            M(0)
            continue
        if name == "V" and ("V", numbers[0]) not in started:
            started.add(("V", numbers[0]))
            VC(0)
        tasks[name](*map(int, numbers))
    for name in list(pending):
        sent(name)
    for copy in outputs:
        copy.wait()


def finish(val, num_out, inbox_out, w_out, mw_out, val_to, num_to, inbox_to, w_to, mw_to, VAL, NUM, INB, sem):
    trips = [(val, VAL, val_to), (num_out, NUM, num_to), (inbox_out, INB, inbox_to)]
    loads = [pltpu.make_async_copy(src, stop, sem.at[i]) for i, (src, stop, dst) in enumerate(trips)]
    stores = [pltpu.make_async_copy(stop, dst, sem.at[3 + i]) for i, (src, stop, dst) in enumerate(trips)]
    for copy in loads:
        copy.start()
    w_to[0] = w_out[0]
    mw_to[0] = mw_out[0]
    for load, store in zip(loads, stores):
        load.wait()
        store.start()
    for copy in stores:
        copy.wait()


def per_device(activations, cotangent, numerator, weight, inbox_num, inbox_wt, lengths, step_index):
    smem, hbm = (pl.BlockSpec(memory_space=m) for m in (pltpu.SMEM, pl.ANY))
    hb = 256 - HA
    matrix = jax.ShapeDtypeStruct((1, 256, HV), F32)
    scalar = jax.ShapeDtypeStruct((1,), F32)
    tokens = jax.ShapeDtypeStruct((2, 1, TOK, HV), BF)
    values, num_out, w_out, inbox_out, mw_out = pl.pallas_call(
        kernel,
        out_shape=(tokens, matrix, scalar, matrix, scalar),
        in_specs=[smem] * 4 + [hbm] * 4,
        out_specs=(hbm, hbm, smem, hbm, smem),
        scratch_shapes=[
            pltpu.VMEM((2, TOK, D), BF),
            pltpu.VMEM((2, 4, 4, 2, 256, HV), BF),
            pltpu.VMEM((4, 4, 2, 256, 256), BF),
            pltpu.VMEM((4, 4, 2, 256, 256), BF),
            pltpu.VMEM((4, 4, 2, 256, 256), BF),
            pltpu.VMEM((2, 2, 4, HA, 256), BF),
            pltpu.VMEM((2, 2, 4, 2, HA, 256), BF),
            pltpu.VMEM((2, 4, HA, 256), BF),
            pltpu.VMEM((2, 4, 4, hb, 256), BF),
            pltpu.VMEM((2, 2, 2, hb, 256), BF),
            pltpu.VMEM((2, 2, 4, hb, 256), BF),
            pltpu.VMEM((2, 2, 2, 256, 256), BF),
            pltpu.VMEM((2, TOK, HV), BF),
            pltpu.VMEM((2, TOK, HV), BF),
            pltpu.VMEM((2, HV, TOK), BF),
            pltpu.VMEM((2, TOK, HV), BF),
            pltpu.VMEM((2, TOK, HV), BF),
            pltpu.VMEM((TOK, HV), F32),
            pltpu.VMEM((2, 256, HV), BF),
            pltpu.VMEM((2, 256, HV), BF),
            pltpu.VMEM((2, 2, 256, HV), BF),
            pltpu.VMEM((256, HV), F32),
            pltpu.VMEM((8, 128), F32),
            pltpu.VMEM((2, 8, 128), F32),
            pltpu.VMEM((2, TOK, HV), BF),
            pltpu.VMEM((256, HV), F32),
            pltpu.VMEM((256, HV), F32),
            pltpu.VMEM((2, 8, 128), F32),
            pltpu.SemaphoreType.DMA((256,)),
            pltpu.SemaphoreType.DMA((256,)),
            pltpu.SemaphoreType.DMA((8,)),
            pltpu.SemaphoreType.REGULAR((4,)),
        ],
        compiler_params=pltpu.CompilerParams(
            collective_id=0, has_side_effects=True, vmem_limit_bytes=63 * 2**20
        ),
        cost_estimate=pl.CostEstimate(flops=4 * 2 * TOK * D * HV, bytes_accessed=2 * TOK * D * 2, transcendentals=0),
        name="push_steps",
    )(step_index, lengths[:, 0, 0], weight, inbox_wt, activations, cotangent, numerator, inbox_num)
    values, num_out, inbox_out, w_out, mw_out = pl.pallas_call(
        finish,
        out_shape=(tokens, matrix, matrix, scalar, scalar),
        in_specs=[hbm] * 3 + [smem] * 2,
        out_specs=(hbm,) * 3 + (smem,) * 2,
        scratch_shapes=[
            pltpu.VMEM((2, 1, TOK, HV), BF),
            pltpu.VMEM((1, 256, HV), F32),
            pltpu.VMEM((1, 256, HV), F32),
            pltpu.SemaphoreType.DMA((6,)),
        ],
        name="finish",
    )(values, num_out, inbox_out, w_out, mw_out)
    return values, num_out, w_out, inbox_out, mw_out


def solution(mesh):
    in_specs = (
        P(None, "rep", "fsdp", None),
        P(None, "rep", "fsdp", None),
        P("rep", "fsdp", None),
        P("rep"),
        P("rep", "fsdp", None),
        P("rep"),
        P(None, "rep", "fsdp"),
        P(),
    )
    out_specs = (
        P(None, "rep", "fsdp", None),
        P("rep", "fsdp", None),
        P("rep"),
        P("rep", "fsdp", None),
        P("rep"),
    )
    return jax.shard_map(
        per_device, mesh=mesh, in_specs=in_specs, out_specs=out_specs, check_vma=False
    )
```

```python
import functools
import math

import jax
import jax.numpy as jnp
from jax import lax
from jax.experimental import pallas as pl
from jax.experimental.pallas import tpu as pltpu
from jax.sharding import PartitionSpec as P

MESH = pl.DeviceIdType.MESH
BF, F32 = jnp.bfloat16, jnp.float32
D, HV, TOK = 8192, 512, 384
INV_ROOT = 1.0 / math.sqrt(D)
HALF_TOK = TOK // 2
ROUTE = 96
HA = 128
SUB = 1024


def kernel(index, length, weight, inbox_wt, act, cot, num, inbox, val, num_out, w_out, inbox_out, mw_out,
           ACT, Z, PT, PS, RSIB, RAH, RAF, RAY, RBY, RBH, RBF, RX, UPL, UP, UPT, VB, VR, VACC,
           ZS, KB, MSG, X1, WT, WR, COT, NUM, INB, RATE, ss, rs, io, credit):
    rep, fs = lax.axis_index("rep"), lax.axis_index("fsdp")
    yh, c = rep // 2, rep % 2
    z, x, yl = fs // 8, (fs // 2) % 4, fs % 2
    q = x % 2
    home = c == q
    guest = c != q
    my = 1 - yl

    def at(core, zz, xx, yy):
        return (yh * 2 + core, lax.rem(zz + 4, 4) * 8 + lax.rem(xx + 4, 4) * 2 + yy)

    sibling, mate = at(1 - c, z, x, yl), at(c, z, x, my)
    up_z, down_z = at(c, z + 1, x, yl), at(c, z + 3, x, yl)
    z0, zp, zm, z2 = z, lax.rem(z + 1, 4), lax.rem(z + 3, 4), lax.rem(z + 2, 4)
    chunk = (z2, zp, zm, z0)
    next1, next2 = (lax.rem(rep + 1, 4), fs), (lax.rem(rep + 2, 4), fs)

    inputs = [pltpu.make_async_copy(*pair, io.at[i])
              for i, pair in enumerate([(num.at[0], NUM), (cot.at[:, 0], COT), (inbox.at[0], INB)])]
    for copy in inputs:
        copy.start()
    names, pending = {}, {}

    def number(name):
        return names.setdefault(name, len(names))

    def remote(name, src, dst, to):
        k = number(name)
        r = number((name[0],) + name[2:]) if name[0].startswith("*") else k
        return pltpu.make_async_remote_copy(src, dst, ss.at[k], rs.at[r], device_id=to, device_id_type=MESH)

    def send(name, src, dst, to, guard=None):
        copy = remote(name, src, dst, to)
        pending[name] = (copy, guard)
        if guard is None:
            copy.start()
        else:
            pl.when(guard)(copy.start)

    def local(name, src, dst, guard):
        r = number((name[0],) + name[2:])
        pl.when(guard)(pltpu.make_async_copy(src, dst, rs.at[r]).start)

    def arrived(name, dst):
        r = number(name)
        pltpu.make_async_copy(dst, dst, rs.at[r]).wait()

    def sent(name):
        copy, guard = pending.pop(name)
        if guard is None:
            copy.wait_send()
        else:
            pl.when(guard)(copy.wait_send)

    def half(h):
        return pl.ds(pl.multiple_of(h * 128, 128), 128)

    rows_a = pl.ds(pl.multiple_of(c * 128, 64), ROUTE)
    rows_b = pl.ds(pl.multiple_of(c * 128 + ROUTE, 16), 128 - ROUTE)
    sib_a = pl.ds(pl.multiple_of((1 - c) * 128, 64), ROUTE)
    sib_b = pl.ds(pl.multiple_of((1 - c) * 128 + ROUTE, 16), 128 - ROUTE)
    hv_a, hv_b = pl.ds(0, HA), pl.ds(HA, 256 - HA)
    low, high, every = pl.ds(0, 2), pl.ds(2, 2), pl.ds(0, 4)
    own, rest = pl.ds(0, 1), pl.ds(1, 3)

    def weight_at(s):
        return weight[0] if s == 0 else 0.5 * weight[0] + inbox_wt[0]

    def project(s):
        block = NUM[...] if s == 0 else X1[...]
        ZS[s] = (block / weight_at(s)).astype(BF)

    def AX(s):
        if s == 1:
            project(s)

        def shard(h, place):
            return ZS.at[s, half(h)], Z.at[s, z, place, yl, half(h)]

        send(("*AXo", 0, s), *shard(1 - c, 0), sibling, home)
        local(("*AXo", 1, s), *shard(c, 0), home)
        far, place = jnp.where(home, x + 2, x + 1), jnp.where(home, 2, 3)
        send(("*AX", 0, s), *shard(0, place), at(0, z, far, yl))
        send(("*AX", 1, s), *shard(1, place), at(1, z, far, yl))
        send(("*AX", 2, s), *shard(0, 1), at(0, z, x + 3, yl), guest)
        send(("*AX", 3, s), *shard(1, 1), at(1, z, x + 3, yl), guest)

    def gathered(s, zz, yy, rows, part=every):
        return Z.at[s, zz, part, yy, rows]

    def pass_on(name, to, zz, yy, rows, source=None, part=every):
        def run(s):
            piece = gathered(s, zz, yy, rows, part)
            if source in ("YZop", "YZom", "YZmp", "YZmm", "ZYy0"):
                both(source, s, zz, yy, rows)
            elif source is not None:
                arrived((source, s), piece)
            send((name, s), piece, piece, to)
        return run

    def both(name, s, zz, yy, rows):
        arrived((name, 0, s), gathered(s, zz, yy, rows, own))
        arrived((name, 1, s), gathered(s, zz, yy, rows, rest))

    def first_hop(plus, minus, rows, part, yy=yl):
        def run(s):
            piece = gathered(s, z, yy, rows, part)
            send((plus, int(part is rest), s), piece, piece, up_z)
            send((minus, int(part is rest), s), piece, piece, down_z)
        return run

    def to_mate(name, rows, part):
        def run(s):
            piece = gathered(s, z, yl, rows, part)
            send((name, int(part is rest), s), piece, piece, mate)
        return run

    def AYp(s):
        arrived(("*AXo", s), gathered(s, z, yl, half(c), own))
        to_mate("YZy", rows_a, own)(s)

    def AYq(s):
        arrived(("*AX", s), gathered(s, z, yl, half(c), rest))
        to_mate("YZy", rows_a, rest)(s)

    def AY1p(s):
        arrived(("YZy", 0, s), gathered(s, z, my, rows_a, own))
        first_hop("YZmp", "YZmm", rows_a, own, my)(s)

    def AY1(s):
        arrived(("YZy", 1, s), gathered(s, z, my, rows_a, rest))
        first_hop("YZmp", "YZmm", rows_a, rest, my)(s)

    def AZa(s):
        both("ZYp", s, zm, yl, rows_b)
        pass_on("ZYfp", up_z, zm, yl, rows_b, None, low)(s)

    def AZb(s):
        both("ZYm", s, zp, yl, rows_b)
        pass_on("ZYfm", down_z, zp, yl, rows_b, None, high)(s)

    def AZc(s):
        arrived(("ZYfp", s), gathered(s, z2, yl, rows_b, low))
        arrived(("ZYfm", s), gathered(s, z2, yl, rows_b, high))
        pass_on("ZYy2", mate, z2, yl, rows_b)(s)

    begun = set()

    def V(s, k):
        zz = chunk[k]
        if s not in begun:
            begun.add(s)
            VACC[...] = jnp.zeros_like(VACC)
        if k == 3:
            arrived(("S0", s), Z.at[s, z, :, yl, half(1 - c)])
            arrived(("S1", s), Z.at[s, z, :, my, sib_a])
            arrived(("Sya", s), Z.at[s, z, :, my, sib_b])
        else:
            four = {2: ("Sa", "Sd", "Sf", "Syb"), 1: ("Sb", "Se", "Sg", "Syc"), 0: ("Sc", "Sh", "Si", "Syd")}[k]
            for name, yy, piece in zip(four, (yl, yl, my, my), (sib_b, sib_a, sib_a, sib_b)):
                arrived((name, s), Z.at[s, zz, :, yy, piece])

        def body(j, carry):
            columns = pl.ds(pl.multiple_of(zz * 2048 + lax.rem(x + j, 4) * 512, 512), 512)
            VACC[...] += jnp.dot(ACT[s, :, columns], Z[s, zz, j].reshape(512, HV), preferred_element_type=F32)
            return carry

        lax.fori_loop(0, 4, body, 0)

    def VRet(s):
        VB[s] = (VACC[...] * INV_ROOT).astype(BF)
        top, low_rows = pl.ds(0, HALF_TOK), pl.ds(HALF_TOK, HALF_TOK)
        send(("*VR", 0, s), VB.at[s, top], VR.at[s, top], at(1 - c, z, x + 3, yl), guest)
        send(("*VR", 1, s), VB.at[s, low_rows], VR.at[s, low_rows], at(1 - c, z, x + 1, yl), guest)
        local(("*VR", 2, s), VB.at[s], VR.at[s], home)

    def valid(s):
        return lax.broadcasted_iota(jnp.int32, (TOK, HV), 0) < length[s]

    def VM(s):
        arrived(("*VR", s), VR.at[s])
        VR[s] = jnp.where(valid(s), VR[s].astype(F32), 0.0).astype(BF)
        result(VR.at[s], val.at[s, 0])

    outputs = []

    def result(src, dst):
        outputs.append(pltpu.make_async_copy(src, dst, io.at[3 + len(outputs)]))
        outputs[-1].start()

    def UPs(s):
        top, low_rows = pl.ds(0, HALF_TOK), pl.ds(HALF_TOK, HALF_TOK)
        send(("*UP", 0, s), UPL.at[s, top], UP.at[s, top], at(1 - c, z, x + 1, yl), guest)
        send(("*UP", 1, s), UPL.at[s, low_rows], UP.at[s, low_rows], at(1 - c, z, x + 3, yl), guest)
        local(("*UP", 2, s), UPL.at[s], UP.at[s], home)

    def UT(s):
        arrived(("*UP", s), UP.at[s])
        mine = UP[s, :, pl.ds(pl.multiple_of(c * 256, 256), 256)]
        UPT[s, 0:256] = mine.astype(F32).T.astype(BF)
        other = UP[s, :, pl.ds(pl.multiple_of((1 - c) * 256, 256), 256)]
        UPT[s, 256:512] = other.astype(F32).T.astype(BF)

    def columns_of(k):
        return pl.ds(pl.multiple_of(chunk[k // 2] * 2048 + (k % 2) * SUB, SUB), SUB)

    def T(s, k):
        cols = columns_of(k)
        for j, to in ((0, x + 1), (1, x + 3)):
            rows = pl.ds(j * HALF_TOK, HALF_TOK)
            send(("*T", j, s, k), act.at[s, 0, rows, cols], ACT.at[s, rows, cols], at(1 - c, z, to, yl), guest)
        local(("*T", 2, s, k), act.at[s, 0, :, cols], ACT.at[s, :, cols], home)

    def C(s, k):
        zz = chunk[k // 2]
        arrived(("*T", s, k), ACT.at[s, :, columns_of(k)])
        if s == 1 and k % 2 == 0:
            used = {0: ("Ahm", "Ahp", "Bhm", "Bhp"), 1: ("Afpo", "Afpm", "Bfpl", "Bfph"),
                    2: ("Afmo", "Afmm", "Bfml", "Bfmh"), 3: ("Ay",)}[k // 2]
            for name in used:
                sent((name, 0))
            sent(("By", 0, k // 2))
            sent(("SIB", 0, k))
            sent(("SIB", 0, k + 1))
            if k == 6:
                for part in range(2):
                    for j in range(4):
                        sent(("*X", j, part, 0))
            pl.semaphore_wait(credit.at[k // 2], 1)

        def body(j, carry):
            cols = pl.ds(pl.multiple_of(zz * 2048 + j * 512, 512), 512)
            block = jnp.dot(UPT[s], ACT[s, :, cols], preferred_element_type=F32).astype(BF)
            for yy in range(2):
                PT[zz, j, yy] = block[0:256, yy * 256:(yy + 1) * 256]
                PS[zz, j, yy] = block[256:512, yy * 256:(yy + 1) * 256]
            return carry

        first = 2 * (k % 2)
        lax.fori_loop(first, first + 2, body, 0)
        pair = pl.ds(first, 2)
        send(("SIB", s, k), PS.at[zz, pair], RSIB.at[zz, pair], sibling)

    def add_into(count, target, *others):
        def body(j, carry):
            total = target(j)[...].astype(F32)
            for other in others:
                total = total + other(j)[...].astype(F32)
            target(j)[...] = total.astype(BF)
            return carry
        lax.fori_loop(0, count, body, 0)

    def Dd(s, k):
        zz = chunk[k]
        arrived(("SIB", s, 2 * k), RSIB.at[zz, low])
        arrived(("SIB", s, 2 * k + 1), RSIB.at[zz, high])
        add_into(8, lambda j: PT.at[zz, j // 2, j % 2], lambda j: RSIB.at[zz, j // 2, j % 2])
        if s == 0:
            pl.semaphore_signal(credit.at[k], inc=1, device_id=sibling, device_id_type=MESH)
        send(("By", s, k), PT.at[zz, :, my, hv_b], RBY.at[s, zz], mate)

    def AH(s):
        send(("Ahm", s), PT.at[z2, :, yl, hv_a], RAH.at[s, 0], down_z)
        send(("Ahp", s), PT.at[z2, :, my, hv_a], RAH.at[s, 1], up_z)

    def Ee(s, k):
        zz = chunk[k]
        arrived(("By", s, k), RBY.at[s, zz])
        add_into(4, lambda j: PT.at[zz, j, yl, hv_b], lambda j: RBY.at[s, zz, j])
        if k == 0:
            send(("Bhm", s), PT.at[zz, low, yl, hv_b], RBH.at[s, 0], down_z)
            send(("Bhp", s), PT.at[zz, high, yl, hv_b], RBH.at[s, 1], up_z)

    def Fmm(s):
        send(("Afmm", s), PT.at[zm, :, my, hv_a], RAF.at[s, 0, :, my], down_z)

    def Fmo(s):
        arrived(("Ahm", s), RAH.at[s, 0])
        add_into(4, lambda j: PT.at[zm, j, yl, hv_a], lambda j: RAH.at[s, 0, j])
        send(("Afmo", s), PT.at[zm, :, yl, hv_a], RAF.at[s, 0, :, yl], down_z)

    def Fpo(s):
        send(("Afpo", s), PT.at[zp, :, yl, hv_a], RAF.at[s, 1, :, yl], up_z)

    def Fpm(s):
        arrived(("Ahp", s), RAH.at[s, 1])
        add_into(4, lambda j: PT.at[zp, j, my, hv_a], lambda j: RAH.at[s, 1, j])
        send(("Afpm", s), PT.at[zp, :, my, hv_a], RAF.at[s, 1, :, my], up_z)

    def Gmh(s):
        send(("Bfmh", s), PT.at[zm, high, yl, hv_b], RBF.at[s, 0, high], down_z)

    def Gml(s):
        arrived(("Bhm", s), RBH.at[s, 0])
        add_into(2, lambda j: PT.at[zm, j, yl, hv_b], lambda j: RBH.at[s, 0, j])
        send(("Bfml", s), PT.at[zm, low, yl, hv_b], RBF.at[s, 0, low], down_z)

    def Gpl(s):
        send(("Bfpl", s), PT.at[zp, low, yl, hv_b], RBF.at[s, 1, low], up_z)

    def Gph(s):
        arrived(("Bhp", s), RBH.at[s, 1])
        add_into(2, lambda j: PT.at[zp, 2 + j, yl, hv_b], lambda j: RBH.at[s, 1, j])
        send(("Bfph", s), PT.at[zp, high, yl, hv_b], RBF.at[s, 1, high], up_z)

    def H(s, yy, minus, plus):
        arrived((minus, s), RAF.at[s, 0, :, yy])
        arrived((plus, s), RAF.at[s, 1, :, yy])
        add_into(4, lambda j: PT.at[z, j, yy, hv_a], lambda j: RAF.at[s, 0, j, yy], lambda j: RAF.at[s, 1, j, yy])

    def Hm(s):
        H(s, my, "Afmm", "Afpm")
        send(("Ay", s), PT.at[z, :, my, hv_a], RAY.at[s], mate)

    def Ho(s):
        H(s, yl, "Afmo", "Afpo")

    def owners(s, part, hv):
        def piece(xx, i):
            xx = lax.rem(xx, 4)
            return PT.at[z, xx, yl, hv], RX.at[s, i, c, hv]

        send(("*X", 0, part, s), *piece(x + 1, 1), at(q, z, x + 1, yl))
        send(("*X", 1, part, s), *piece(x + 3, 0), at(q, z, x + 3, yl))
        send(("*X", 2, part, s), *piece(x + 2, 1), at(q, z, x + 2, yl))
        send(("*X", 3, part, s), *piece(x, 0), sibling, guest)
        local(("*X", 4, part, s), *piece(x, 0), home)

    def I(s):
        arrived(("Ay", s), RAY.at[s])
        add_into(4, lambda j: PT.at[z, j, yl, hv_a], lambda j: RAY.at[s, j])
        owners(s, 0, hv_a)

    def J(s):
        for name, way, part in (("Bfml", 0, low), ("Bfmh", 0, high), ("Bfpl", 1, low), ("Bfph", 1, high)):
            arrived((name, s), RBF.at[s, way, part])
        add_into(4, lambda j: PT.at[z, j, yl, hv_b], lambda j: RBF.at[s, 0, j], lambda j: RBF.at[s, 1, j])
        owners(s, 1, hv_b)

    def chosen(s, part):
        return jnp.where(jnp.full((256, 256), index[s] % 2) == 0, MSG[s, 0, part].astype(F32),
                         MSG[s, 1, part].astype(F32))

    def U(s, part, hv):
        arrived(("*X", part, s), RX.at[s, :, :, hv])
        if s == 1:
            for j in range(2):
                arrived(("MSG", j, part, 0), MSG.at[0, j, part])
            message = chosen(0, part)
        for h in range(2):
            mine, cols = slice(h * 128, (h + 1) * 128), slice(h * 256 + part * 128, h * 256 + (part + 1) * 128)
            grad = (RX[s, 0, h, hv].astype(F32) + RX[s, 1, h, hv].astype(F32)).T
            block = NUM[:, cols] if s == 0 else X1[:, cols]
            kept = 0.5 * (block - RATE[s, 0:1, 0:1] * grad)
            KB[s, part, :, mine] = kept.astype(BF)
            X1[:, cols] = kept + (INB[:, cols] if s == 0 else message[:, mine])

    def UA(s):
        U(s, 0, hv_a)

    def UB(s):
        U(s, 1, hv_b)

    def MS(s, part):
        send(("MSG", 0, part, s), KB.at[s, part], MSG.at[s, 0, part], next1)
        send(("MSG", 1, part, s), KB.at[s, part], MSG.at[s, 1, part], next2)

    def MSA(s):
        MS(s, 0)

    def MSB(s):
        MS(s, 1)

    def M(s):
        result(X1, num_out.at[0])
        for j in range(2):
            arrived(("WT", j), WR.at[j])
        even0, even1 = index[0] % 2 == 0, index[1] % 2 == 0
        w_out[0] = 0.5 * weight_at(1) + 0.5 * jnp.where(even0, WR[0, 0, 0], WR[1, 0, 0])
        mw_out[0] = 0.5 * (0.5 * jnp.where(even1, WR[0, 0, 0], WR[1, 0, 0])
                           + jnp.where(even1, WR[0, 4, 0], WR[1, 4, 0]))
        for part in range(2):
            for j in range(2):
                arrived(("MSG", j, part, 1), MSG.at[1, j, part])
            message = chosen(1, part)
            for h in range(2):
                cols = slice(h * 256 + part * 128, h * 256 + (part + 1) * 128)
                INB[:, cols] = message[:, h * 128:(h + 1) * 128]
        result(INB, inbox_out.at[0])

    AYzp, AYzq = first_hop("ZYp", "ZYm", rows_b, own), first_hop("ZYp", "ZYm", rows_b, rest)
    AYop, AYoq = first_hop("YZop", "YZom", rows_a, own), first_hop("YZop", "YZom", rows_a, rest)
    AYnp, AYnq = to_mate("ZYy0", rows_b, own), to_mate("ZYy0", rows_b, rest)
    AZay, AZby = pass_on("ZYym", mate, zm, yl, rows_b), pass_on("ZYyp", mate, zp, yl, rows_b)
    AZd = pass_on("YZfp", up_z, zm, yl, rows_a, "YZop")
    AZg = pass_on("YZfm", down_z, zp, my, rows_a, "YZmm")
    FS0, FS1 = pass_on("S0", sibling, z, yl, half(c)), pass_on("S1", sibling, z, my, rows_a)
    FSa, FSb = pass_on("Sa", sibling, zm, yl, rows_b), pass_on("Sb", sibling, zp, yl, rows_b)
    FSc, FSd = pass_on("Sc", sibling, z2, yl, rows_b), pass_on("Sd", sibling, zm, yl, rows_a)
    FSe, FSf = pass_on("Se", sibling, zp, yl, rows_a, "YZom"), pass_on("Sf", sibling, zm, my, rows_a, "YZmp")
    FSg, FSh = pass_on("Sg", sibling, zp, my, rows_a), pass_on("Sh", sibling, z2, yl, rows_a, "YZfp")
    FSi, FSya = pass_on("Si", sibling, z2, my, rows_a, "YZfm"), pass_on("Sya", sibling, z0, my, rows_b, "ZYy0")
    FSyb, FSyc = pass_on("Syb", sibling, zm, my, rows_b, "ZYym"), pass_on("Syc", sibling, zp, my, rows_b, "ZYyp")
    FSyd = pass_on("Syd", sibling, z2, my, rows_b, "ZYy2")

    barrier = pltpu.get_barrier_semaphore()
    others = [(lax.rem(rep + j, 4), fs) for j in (1, 2, 3)] + [mate, up_z, down_z]
    others += [at(core, z, x + j, yl) for core in (0, 1) for j in (1, 2, 3)]
    for other in others:
        pl.semaphore_signal(barrier, inc=1, device_id=other, device_id_type=MESH)
    WT[...] = jnp.where(lax.broadcasted_iota(jnp.int32, (8, 128), 0) < 4, weight[0], inbox_wt[0])
    for s in range(2):
        step = jnp.full((8, 128), index[s]).astype(F32)
        RATE[s] = 0.5 * math.sqrt(D / (TOK * 32)) * INV_ROOT * (1.0 + 0.5 * jnp.cos(jnp.pi * step / 1024.0))
    inputs[0].wait()
    project(0)
    inputs[1].wait()
    for s in range(2):
        UPL[s] = jnp.where(valid(s), COT[s].astype(F32), 0.0).astype(BF)
    inputs[2].wait()
    pl.semaphore_wait(barrier, len(others))

    send(("WT", 0), WT, WR.at[0], next1)
    send(("WT", 1), WT, WR.at[1], next2)
    for task, *numbers in (
        (UPs, 0), (AX, 0), (T, 0, 0), (AYp, 0), (AYop, 0), (AYzp, 0), (AY1p, 0), (T, 0, 1), (T, 0, 2), (AYq, 0),
        (AYzq, 0), (AZa, 0), (T, 0, 3), (UT, 0), (AYoq, 0), (T, 0, 4), (AZb, 0), (C, 0, 0), (AZay, 0), (AY1, 0),
        (FS1, 0), (C, 0, 1), (T, 0, 5), (C, 0, 2), (Dd, 0, 0), (T, 0, 6), (C, 0, 3), (T, 0, 7), (AH, 0), (T, 1, 0),
        (UPs, 1), (AYnp, 0), (AZc, 0), (C, 0, 4), (Dd, 0, 1), (C, 0, 5), (Ee, 0, 0), (FS0, 0), (Fpm, 0), (T, 1, 1),
        (Dd, 0, 2), (Fmm, 0), (Fpo, 0), (C, 0, 6), (Fmo, 0), (AYnq, 0), (FSyb, 0), (C, 0, 7), (Dd, 0, 3), (T, 1, 2),
        (Ee, 0, 1), (Ee, 0, 2), (Gph, 0), (UT, 1), (Gml, 0), (Gpl, 0), (Gmh, 0), (Hm, 0), (AZd, 0), (FSd, 0),
        (C, 1, 0), (AZg, 0), (C, 1, 1), (FSb, 0), (T, 1, 3), (AZby, 0), (Dd, 1, 0), (AH, 1), (Ho, 0), (Ee, 0, 3),
        (J, 0), (C, 1, 2), (I, 0), (C, 1, 3), (FSc, 0), (FSyc, 0), (FSf, 0), (FSya, 0), (UB, 0), (Dd, 1, 1),
        (UA, 0), (AX, 1), (Ee, 1, 0), (AYp, 1), (MSB, 0), (AYzp, 1), (Fpm, 1), (FSh, 0), (AYop, 1), (T, 1, 4),
        (T, 1, 5), (Ee, 1, 1), (AYq, 1), (AYzq, 1), (Gpl, 1), (AYoq, 1), (FSe, 0), (C, 1, 4), (FSyd, 0), (T, 1, 6),
        (FSa, 0), (T, 1, 7), (AY1p, 1), (AZb, 1), (AYnq, 1), (C, 1, 5), (AZa, 1), (AY1, 1), (FSa, 1), (Gph, 1),
        (AZby, 1), (Fpo, 1), (FSb, 1), (AZay, 1), (FSg, 0), (V, 0, 2), (Dd, 1, 2), (C, 1, 6), (FSe, 1), (AYnp, 1),
        (Fmm, 1), (C, 1, 7), (Dd, 1, 3), (Fmo, 1), (V, 0, 1), (AZd, 1), (FSd, 1), (AZc, 1), (FS1, 1), (Ee, 1, 2),
        (FSc, 1), (FSf, 1), (FSyb, 1), (Hm, 1), (FS0, 1), (Gml, 1), (Gmh, 1), (MSA, 0), (AZg, 1), (FSi, 0),
        (V, 0, 3), (Ee, 1, 3), (V, 0, 0), (FSg, 1), (VRet, 0), (V, 1, 2), (J, 1), (Ho, 1), (FSyd, 1), (FSyc, 1),
        (FSya, 1), (I, 1), (V, 1, 1), (UB, 1), (MSB, 1), (FSh, 1), (FSi, 1), (UA, 1), (MSA, 1), (V, 1, 3), (VM, 0),
        (V, 1, 0), (VRet, 1), (VM, 1), (M, 0),
    ):
        task(*numbers)
    for name in list(pending):
        sent(name)
    for copy in outputs:
        copy.wait()


def finish(val, num_out, inbox_out, w_out, mw_out, val_to, num_to, inbox_to, w_to, mw_to, VAL, NUM, INB, sem):
    trips = [(val, VAL, val_to), (num_out, NUM, num_to), (inbox_out, INB, inbox_to)]
    loads = [pltpu.make_async_copy(src, stop, sem.at[i]) for i, (src, stop, dst) in enumerate(trips)]
    stores = [pltpu.make_async_copy(stop, dst, sem.at[3 + i]) for i, (src, stop, dst) in enumerate(trips)]
    for copy in loads:
        copy.start()
    w_to[0] = w_out[0]
    mw_to[0] = mw_out[0]
    for load, store in zip(loads, stores):
        load.wait()
        store.start()
    for copy in stores:
        copy.wait()


def per_device(activations, cotangent, numerator, weight, inbox_num, inbox_wt, lengths, step_index):
    smem, hbm = (pl.BlockSpec(memory_space=m) for m in (pltpu.SMEM, pl.ANY))
    hb = 256 - HA
    matrix = jax.ShapeDtypeStruct((1, 256, HV), F32)
    scalar = jax.ShapeDtypeStruct((1,), F32)
    tokens = jax.ShapeDtypeStruct((2, 1, TOK, HV), BF)
    values, num_out, w_out, inbox_out, mw_out = pl.pallas_call(
        kernel,
        out_shape=(tokens, matrix, scalar, matrix, scalar),
        in_specs=[smem] * 4 + [hbm] * 4,
        out_specs=(hbm, hbm, smem, hbm, smem),
        scratch_shapes=[
            pltpu.VMEM((2, TOK, D), BF),
            pltpu.VMEM((2, 4, 4, 2, 256, HV), BF),
            pltpu.VMEM((4, 4, 2, 256, 256), BF),
            pltpu.VMEM((4, 4, 2, 256, 256), BF),
            pltpu.VMEM((4, 4, 2, 256, 256), BF),
            pltpu.VMEM((2, 2, 4, HA, 256), BF),
            pltpu.VMEM((2, 2, 4, 2, HA, 256), BF),
            pltpu.VMEM((2, 4, HA, 256), BF),
            pltpu.VMEM((2, 4, 4, hb, 256), BF),
            pltpu.VMEM((2, 2, 2, hb, 256), BF),
            pltpu.VMEM((2, 2, 4, hb, 256), BF),
            pltpu.VMEM((2, 2, 2, 256, 256), BF),
            pltpu.VMEM((2, TOK, HV), BF),
            pltpu.VMEM((2, TOK, HV), BF),
            pltpu.VMEM((2, HV, TOK), BF),
            pltpu.VMEM((2, TOK, HV), BF),
            pltpu.VMEM((2, TOK, HV), BF),
            pltpu.VMEM((TOK, HV), F32),
            pltpu.VMEM((2, 256, HV), BF),
            pltpu.VMEM((2, 2, 256, 256), BF),
            pltpu.VMEM((2, 2, 2, 256, 256), BF),
            pltpu.VMEM((256, HV), F32),
            pltpu.VMEM((8, 128), F32),
            pltpu.VMEM((2, 8, 128), F32),
            pltpu.VMEM((2, TOK, HV), BF),
            pltpu.VMEM((256, HV), F32),
            pltpu.VMEM((256, HV), F32),
            pltpu.VMEM((2, 8, 128), F32),
            pltpu.SemaphoreType.DMA((256,)),
            pltpu.SemaphoreType.DMA((256,)),
            pltpu.SemaphoreType.DMA((8,)),
            pltpu.SemaphoreType.REGULAR((4,)),
        ],
        compiler_params=pltpu.CompilerParams(
            collective_id=0, has_side_effects=True, vmem_limit_bytes=63 * 2**20
        ),
        cost_estimate=pl.CostEstimate(flops=4 * 2 * TOK * D * HV, bytes_accessed=2 * TOK * D * 2, transcendentals=0),
        name="push_steps",
    )(step_index, lengths[:, 0, 0], weight, inbox_wt, activations, cotangent, numerator, inbox_num)
    values, num_out, inbox_out, w_out, mw_out = pl.pallas_call(
        finish,
        out_shape=(tokens, matrix, matrix, scalar, scalar),
        in_specs=[hbm] * 3 + [smem] * 2,
        out_specs=(hbm,) * 3 + (smem,) * 2,
        scratch_shapes=[
            pltpu.VMEM((2, 1, TOK, HV), BF),
            pltpu.VMEM((1, 256, HV), F32),
            pltpu.VMEM((1, 256, HV), F32),
            pltpu.SemaphoreType.DMA((6,)),
        ],
        name="finish",
    )(values, num_out, inbox_out, w_out, mw_out)
    return values, num_out, w_out, inbox_out, mw_out


def solution(mesh):
    in_specs = (
        P(None, "rep", "fsdp", None),
        P(None, "rep", "fsdp", None),
        P("rep", "fsdp", None),
        P("rep"),
        P("rep", "fsdp", None),
        P("rep"),
        P(None, "rep", "fsdp"),
        P(),
    )
    out_specs = (
        P(None, "rep", "fsdp", None),
        P("rep", "fsdp", None),
        P("rep"),
        P("rep", "fsdp", None),
        P("rep"),
    )
    return jax.shard_map(
        per_device, mesh=mesh, in_specs=in_specs, out_specs=out_specs, check_vma=False
    )
```

```python
import functools
import math

import jax
import jax.numpy as jnp
from jax import lax
from jax.experimental import pallas as pl
from jax.experimental.pallas import tpu as pltpu
from jax.sharding import PartitionSpec as P

MESH = pl.DeviceIdType.MESH
BF, F32 = jnp.bfloat16, jnp.float32
D, HV, TOK = 8192, 512, 384
INV_ROOT = 1.0 / math.sqrt(D)
HALF_TOK = TOK // 2
ROUTE = 96
HA = 128


def kernel(index_at, length_at, weight_at_, inbox_wt_at, act, cot, num, inbox, val, num_out, w_out, inbox_out, mw_out,
           ACT, Z, PT, PS, RSIB, RAH, RAF, RAY, RBY, RBH, RBF, RX, UPL, UP, UPT, VB, VR, VACC,
           ZS, KB, MSG, X1, WT, WR, COT, NUM, INB, RATE, index, length, weight, inbox_wt, wts0, wts1, ss, rs, io, credit):
    rep, fs = lax.axis_index("rep"), lax.axis_index("fsdp")
    yh, c = rep // 2, rep % 2
    z, x, yl = fs // 8, (fs // 2) % 4, fs % 2
    q = x % 2
    home = c == q
    guest = c != q
    my = 1 - yl

    def at(core, zz, xx, yy):
        return (yh * 2 + core, lax.rem(zz + 4, 4) * 8 + lax.rem(xx + 4, 4) * 2 + yy)

    sibling, mate = at(1 - c, z, x, yl), at(c, z, x, my)
    up_z, down_z = at(c, z + 1, x, yl), at(c, z + 3, x, yl)
    z0, zp, zm, z2 = z, lax.rem(z + 1, 4), lax.rem(z + 3, 4), lax.rem(z + 2, 4)
    chunk = (z2, zp, zm, z0)
    parts = ((z2, 0), (z2, 1), (zp, 0), (zm, 0), (zp, 1), (zm, 1), (z0, 0), (z0, 1))
    next1, next2 = (lax.rem(rep + 1, 4), fs), (lax.rem(rep + 2, 4), fs)

    inputs = [pltpu.make_async_copy(*pair, io.at[i])
              for i, pair in enumerate([(num.at[0], NUM), (cot.at[:, 0], COT), (inbox.at[0], INB)])]
    numbers_in = [pltpu.make_async_copy(*pair, io.at[3 + i]) for i, pair in enumerate(
        [(index_at, index), (length_at, length), (weight_at_, weight), (inbox_wt_at, inbox_wt)])]
    for copy in numbers_in + inputs:
        copy.start()
    names, pending = {}, {}

    def number(name):
        return names.setdefault(name, len(names))

    def remote(name, src, dst, to):
        k = number(name)
        r = number((name[0],) + name[2:]) if name[0].startswith("*") else k
        return pltpu.make_async_remote_copy(src, dst, ss.at[k], rs.at[r], device_id=to, device_id_type=MESH)

    def send(name, src, dst, to, guard=None):
        copy = remote(name, src, dst, to)
        pending[name] = (copy, guard)
        if guard is None:
            copy.start()
        else:
            pl.when(guard)(copy.start)

    def local(name, src, dst, guard):
        r = number((name[0],) + name[2:])
        pl.when(guard)(pltpu.make_async_copy(src, dst, rs.at[r]).start)

    def arrived(name, dst):
        r = number(name)
        pltpu.make_async_copy(dst, dst, rs.at[r]).wait()

    def sent(name):
        copy, guard = pending.pop(name)
        if guard is None:
            copy.wait_send()
        else:
            pl.when(guard)(copy.wait_send)

    def half(h):
        return pl.ds(pl.multiple_of(h * 128, 128), 128)

    rows_a = pl.ds(pl.multiple_of(c * 128, 64), ROUTE)
    rows_b = pl.ds(pl.multiple_of(c * 128 + ROUTE, 16), 128 - ROUTE)
    sib_a = pl.ds(pl.multiple_of((1 - c) * 128, 64), ROUTE)
    sib_b = pl.ds(pl.multiple_of((1 - c) * 128 + ROUTE, 16), 128 - ROUTE)
    hv_a, hv_b = pl.ds(0, HA), pl.ds(HA, 256 - HA)
    low, high, every = pl.ds(0, 2), pl.ds(2, 2), pl.ds(0, 4)
    pairs = (low, high)
    own, rest = pl.ds(0, 1), pl.ds(1, 3)

    def weight_at(s):
        return weight[0] if s == 0 else 0.5 * weight[0] + inbox_wt[0]

    def project(s):
        block = NUM[...] if s == 0 else X1[...]
        ZS[s] = (block / weight_at(s)).astype(BF)

    def AX(s):
        if s == 1:
            project(s)

        def shard(h, place):
            return ZS.at[s, half(h)], Z.at[s, z, place, yl, half(h)]

        send(("*AXo", 0, s), *shard(1 - c, 0), sibling, home)
        local(("*AXo", 1, s), *shard(c, 0), home)
        far, place = jnp.where(home, x + 2, x + 1), jnp.where(home, 2, 3)
        send(("*AX", 0, s), *shard(0, place), at(0, z, far, yl))
        send(("*AX", 1, s), *shard(1, place), at(1, z, far, yl))
        send(("*AX", 2, s), *shard(0, 1), at(0, z, x + 3, yl), guest)
        send(("*AX", 3, s), *shard(1, 1), at(1, z, x + 3, yl), guest)

    def gathered(s, zz, yy, rows, part=every):
        return Z.at[s, zz, part, yy, rows]

    def pass_on(name, to, zz, yy, rows, source=None, part=every):
        def run(s):
            piece = gathered(s, zz, yy, rows, part)
            if source in ("YZop", "YZom", "YZmp", "YZmm", "ZYy0"):
                both(source, s, zz, yy, rows)
            elif source is not None:
                arrived((source, s), piece)
            send((name, s), piece, piece, to)
        return run

    def both(name, s, zz, yy, rows):
        arrived((name, 0, s), gathered(s, zz, yy, rows, own))
        arrived((name, 1, s), gathered(s, zz, yy, rows, rest))

    def first_hop(plus, minus, rows, part, yy=yl):
        def run(s):
            piece = gathered(s, z, yy, rows, part)
            send((plus, int(part is rest), s), piece, piece, up_z)
            send((minus, int(part is rest), s), piece, piece, down_z)
        return run

    def to_mate(name, rows, part):
        def run(s):
            piece = gathered(s, z, yl, rows, part)
            send((name, int(part is rest), s), piece, piece, mate)
        return run

    def AYp(s):
        arrived(("*AXo", s), gathered(s, z, yl, half(c), own))
        to_mate("YZy", rows_a, own)(s)

    def AYq(s):
        arrived(("*AX", s), gathered(s, z, yl, half(c), rest))
        to_mate("YZy", rows_a, rest)(s)

    def AY1p(s):
        arrived(("YZy", 0, s), gathered(s, z, my, rows_a, own))
        first_hop("YZmp", "YZmm", rows_a, own, my)(s)

    def AY1(s):
        arrived(("YZy", 1, s), gathered(s, z, my, rows_a, rest))
        first_hop("YZmp", "YZmm", rows_a, rest, my)(s)

    def AZa(s):
        both("ZYp", s, zm, yl, rows_b)
        pass_on("ZYfp", up_z, zm, yl, rows_b, None, low)(s)

    def AZb(s):
        both("ZYm", s, zp, yl, rows_b)
        pass_on("ZYfm", down_z, zp, yl, rows_b, None, high)(s)

    def AZc(s):
        arrived(("ZYfp", s), gathered(s, z2, yl, rows_b, low))
        arrived(("ZYfm", s), gathered(s, z2, yl, rows_b, high))
        pass_on("ZYy2", mate, z2, yl, rows_b)(s)

    begun = set()

    def V(s, k):
        zz = chunk[k]
        if s not in begun:
            begun.add(s)
            VACC[...] = jnp.zeros_like(VACC)
        if k == 3:
            arrived(("S0", s), Z.at[s, z, :, yl, half(1 - c)])
            arrived(("S1", s), Z.at[s, z, :, my, sib_a])
            arrived(("Sya", s), Z.at[s, z, :, my, sib_b])
        else:
            four = {2: ("Sa", "Sd", "Sf", "Syb"), 1: ("Sb", "Se", "Sg", "Syc"), 0: ("Sc", "Sh", "Si", "Syd")}[k]
            for name, yy, piece in zip(four, (yl, yl, my, my), (sib_b, sib_a, sib_a, sib_b)):
                arrived((name, s), Z.at[s, zz, :, yy, piece])

        def body(j, carry):
            columns = pl.ds(pl.multiple_of(zz * 2048 + lax.rem(x + j, 4) * 512, 512), 512)
            VACC[...] += jnp.dot(ACT[s, :, columns], Z[s, zz, j].reshape(512, HV), preferred_element_type=F32)
            return carry

        lax.fori_loop(0, 4, body, 0)

    def VRet(s):
        VB[s] = (VACC[...] * INV_ROOT).astype(BF)
        top, low_rows = pl.ds(0, HALF_TOK), pl.ds(HALF_TOK, HALF_TOK)
        send(("*VR", 0, s), VB.at[s, top], VR.at[s, top], at(1 - c, z, x + 3, yl), guest)
        send(("*VR", 1, s), VB.at[s, low_rows], VR.at[s, low_rows], at(1 - c, z, x + 1, yl), guest)
        local(("*VR", 2, s), VB.at[s], VR.at[s], home)

    def valid(s):
        return lax.broadcasted_iota(jnp.int32, (TOK, HV), 0) < length[s]

    def VM(s):
        arrived(("*VR", s), VR.at[s])
        VR[s] = jnp.where(valid(s), VR[s].astype(F32), 0.0).astype(BF)
        result(VR.at[s], val.at[s, 0])

    outputs = []

    def result(src, dst):
        outputs.append(pltpu.make_async_copy(src, dst, io.at[7 + len(outputs)]))
        outputs[-1].start()

    def UPs(s):
        top, low_rows = pl.ds(0, HALF_TOK), pl.ds(HALF_TOK, HALF_TOK)
        send(("*UP", 0, s), UPL.at[s, top], UP.at[s, top], at(1 - c, z, x + 1, yl), guest)
        send(("*UP", 1, s), UPL.at[s, low_rows], UP.at[s, low_rows], at(1 - c, z, x + 3, yl), guest)
        local(("*UP", 2, s), UPL.at[s], UP.at[s], home)

    def UT(s):
        arrived(("*UP", s), UP.at[s])
        mine = UP[s, :, pl.ds(pl.multiple_of(c * 256, 256), 256)]
        UPT[s, 0:256] = mine.astype(F32).T.astype(BF)
        other = UP[s, :, pl.ds(pl.multiple_of((1 - c) * 256, 256), 256)]
        UPT[s, 256:512] = other.astype(F32).T.astype(BF)

    def columns_of(zz, xx):
        return pl.ds(pl.multiple_of(zz * 2048 + lax.rem(xx, 4) * 512, 512), 512)

    def T(s, k):
        zz, h = parts[k]
        for e in (2 * h, 2 * h + 1):
            for j, to in ((0, x + 1), (1, x + 3)):
                rows, cols = pl.ds(j * HALF_TOK, HALF_TOK), columns_of(zz, to + e)
                send(("*T", 4 * j + e, s, k), act.at[s, 0, rows, cols], ACT.at[s, rows, cols],
                     at(1 - c, z, to, yl), guest)
            cols = columns_of(zz, x + e)
            local(("*T", 8 + e, s, k), act.at[s, 0, :, cols], ACT.at[s, :, cols], home)

    def C(s, k):
        zz, h = parts[k]
        arrived(("*T", s, k), ACT.at[s, :, pl.ds(0, 1024)])
        if s == 1:
            used = (("Ahm", "Bhm"), ("Ahp", "Bhp"), ("Afpl", "Bfpl"), ("Afml", "Bfml"), ("Afph", "Bfph"),
                    ("Afmh", "Bfmh"), ("Ayl",), ("Ayh",))[k]
            for name in used:
                sent((name, 0))
            sent(("By", 0, k))
            sent(("SIB", 0, k))
            if k >= 6:
                for part in range(2):
                    for j in (2 * h, 2 * h + 1):
                        sent(("*X", j, part, 0))
            pl.semaphore_wait(credit.at[k], 1)

        def body(j, carry):
            block = jnp.dot(UPT[s], ACT[s, :, columns_of(zz, x + j)], preferred_element_type=F32).astype(BF)
            for yy in range(2):
                PT[zz, j, yy] = block[0:256, yy * 256:(yy + 1) * 256]
                PS[zz, j, yy] = block[256:512, yy * 256:(yy + 1) * 256]
            return carry

        lax.fori_loop(2 * h, 2 * h + 2, body, 0)
        send(("SIB", s, k), PS.at[zz, pairs[h]], RSIB.at[zz, pairs[h]], sibling)

    def add_into(count, target, *others):
        def body(j, carry):
            total = target(j)[...].astype(F32)
            for other in others:
                total = total + other(j)[...].astype(F32)
            target(j)[...] = total.astype(BF)
            return carry
        lax.fori_loop(0, count, body, 0)

    def Dd(s, k):
        zz, h = parts[k]
        arrived(("SIB", s, k), RSIB.at[zz, pairs[h]])
        add_into(4, lambda j: PT.at[zz, 2 * h + j // 2, j % 2], lambda j: RSIB.at[zz, 2 * h + j // 2, j % 2])
        if s == 0:
            pl.semaphore_signal(credit.at[k], inc=1, device_id=sibling, device_id_type=MESH)
        send(("By", s, k), PT.at[zz, pairs[h], my, hv_b], RBY.at[s, zz, pairs[h]], mate)

    def Ee(s, k):
        zz, h = parts[k]
        arrived(("By", s, k), RBY.at[s, zz, pairs[h]])
        add_into(2, lambda j: PT.at[zz, 2 * h + j, yl, hv_b], lambda j: RBY.at[s, zz, 2 * h + j])
        if k == 0:
            send(("Bhm", s), PT.at[zz, low, yl, hv_b], RBH.at[s, 0], down_z)
        if k == 1:
            send(("Bhp", s), PT.at[zz, high, yl, hv_b], RBH.at[s, 1], up_z)

    def AHm(s):
        send(("Ahm", s), PT.at[z2, low, :, hv_a], RAH.at[s, 0], down_z)

    def AHp(s):
        send(("Ahp", s), PT.at[z2, high, :, hv_a], RAH.at[s, 1], up_z)

    def Fml(s):
        arrived(("Ahm", s), RAH.at[s, 0])
        add_into(4, lambda j: PT.at[zm, j // 2, j % 2, hv_a], lambda j: RAH.at[s, 0, j // 2, j % 2])
        send(("Afml", s), PT.at[zm, low, :, hv_a], RAF.at[s, 0, low], down_z)

    def Fmh(s):
        send(("Afmh", s), PT.at[zm, high, :, hv_a], RAF.at[s, 0, high], down_z)

    def Fpl(s):
        send(("Afpl", s), PT.at[zp, low, :, hv_a], RAF.at[s, 1, low], up_z)

    def Fph(s):
        arrived(("Ahp", s), RAH.at[s, 1])
        add_into(4, lambda j: PT.at[zp, 2 + j // 2, j % 2, hv_a], lambda j: RAH.at[s, 1, j // 2, j % 2])
        send(("Afph", s), PT.at[zp, high, :, hv_a], RAF.at[s, 1, high], up_z)

    def Gmh(s):
        send(("Bfmh", s), PT.at[zm, high, yl, hv_b], RBF.at[s, 0, high], down_z)

    def Gml(s):
        arrived(("Bhm", s), RBH.at[s, 0])
        add_into(2, lambda j: PT.at[zm, j, yl, hv_b], lambda j: RBH.at[s, 0, j])
        send(("Bfml", s), PT.at[zm, low, yl, hv_b], RBF.at[s, 0, low], down_z)

    def Gpl(s):
        send(("Bfpl", s), PT.at[zp, low, yl, hv_b], RBF.at[s, 1, low], up_z)

    def Gph(s):
        arrived(("Bhp", s), RBH.at[s, 1])
        add_into(2, lambda j: PT.at[zp, 2 + j, yl, hv_b], lambda j: RBH.at[s, 1, j])
        send(("Bfph", s), PT.at[zp, high, yl, hv_b], RBF.at[s, 1, high], up_z)

    def H(s, h, minus, plus, name):
        arrived((minus, s), RAF.at[s, 0, pairs[h]])
        arrived((plus, s), RAF.at[s, 1, pairs[h]])
        add_into(4, lambda j: PT.at[z, 2 * h + j // 2, j % 2, hv_a], lambda j: RAF.at[s, 0, 2 * h + j // 2, j % 2],
                 lambda j: RAF.at[s, 1, 2 * h + j // 2, j % 2])
        send((name, s), PT.at[z, pairs[h], my, hv_a], RAY.at[s, pairs[h]], mate)

    def Hl(s):
        H(s, 0, "Afml", "Afpl", "Ayl")

    def Hh(s):
        H(s, 1, "Afmh", "Afph", "Ayh")

    def owners(s, part, hv, h):
        def piece(place, i):
            return PT.at[z, place, yl, hv], RX.at[s, i, c, hv]

        if h == 0:
            send(("*X", 1, part, s), *piece(1, 1), at(q, z, x + 1, yl))
            send(("*X", 0, part, s), *piece(0, 0), sibling, guest)
            local(("*X", 4, part, s), *piece(0, 0), home)
        else:
            send(("*X", 2, part, s), *piece(2, 1), at(q, z, x + 2, yl))
            send(("*X", 3, part, s), *piece(3, 0), at(q, z, x + 3, yl))

    def I(s, h, name):
        arrived((name, s), RAY.at[s, pairs[h]])
        add_into(2, lambda j: PT.at[z, 2 * h + j, yl, hv_a], lambda j: RAY.at[s, 2 * h + j])
        owners(s, 0, hv_a, h)

    def Il(s):
        I(s, 0, "Ayl")

    def Ih(s):
        I(s, 1, "Ayh")

    def J(s, h, minus, plus):
        arrived((minus, s), RBF.at[s, 0, pairs[h]])
        arrived((plus, s), RBF.at[s, 1, pairs[h]])
        add_into(2, lambda j: PT.at[z, 2 * h + j, yl, hv_b], lambda j: RBF.at[s, 0, 2 * h + j],
                 lambda j: RBF.at[s, 1, 2 * h + j])
        owners(s, 1, hv_b, h)

    def Jl(s):
        J(s, 0, "Bfml", "Bfpl")

    def Jh(s):
        J(s, 1, "Bfmh", "Bfph")

    def chosen(s, part):
        return jnp.where(jnp.full((256, 256), index[s] % 2) == 0, MSG[s, 0, part].astype(F32),
                         MSG[s, 1, part].astype(F32))

    def U(s, part, hv):
        arrived(("*X", part, s), RX.at[s, :, :, hv])
        if s == 1:
            for j in range(2):
                arrived(("MSG", j, part, 0), MSG.at[0, j, part])
            message = chosen(0, part)
        for h in range(2):
            mine, cols = slice(h * 128, (h + 1) * 128), slice(h * 256 + part * 128, h * 256 + (part + 1) * 128)
            grad = (RX[s, 0, h, hv].astype(F32) + RX[s, 1, h, hv].astype(F32)).T
            block = NUM[:, cols] if s == 0 else X1[:, cols]
            kept = 0.5 * (block - RATE[s, 0:1, 0:1] * grad)
            KB[s, part, :, mine] = kept.astype(BF)
            X1[:, cols] = kept + (INB[:, cols] if s == 0 else message[:, mine])

    def weights():
        for j in range(2):
            arrived(("WT", j), WR.at[j])
        even0, even1 = index[0] % 2 == 0, index[1] % 2 == 0
        wts0[0] = 0.5 * weight_at(1) + 0.5 * jnp.where(even0, WR[0, 0, 0], WR[1, 0, 0])
        wts1[0] = 0.5 * (0.5 * jnp.where(even1, WR[0, 0, 0], WR[1, 0, 0])
                           + jnp.where(even1, WR[0, 4, 0], WR[1, 4, 0]))
        result(wts0, w_out)
        result(wts1, mw_out)

    def UA(s):
        U(s, 0, hv_a)
        if s == 0:
            weights()

    def UB(s):
        U(s, 1, hv_b)

    def MS(s, part):
        send(("MSG", 0, part, s), KB.at[s, part], MSG.at[s, 0, part], next1)
        send(("MSG", 1, part, s), KB.at[s, part], MSG.at[s, 1, part], next2)

    def MSA(s):
        MS(s, 0)

    def MSB(s):
        MS(s, 1)

    def M(s):
        result(X1, num_out.at[0])
        for part in range(2):
            for j in range(2):
                arrived(("MSG", j, part, 1), MSG.at[1, j, part])
            message = chosen(1, part)
            for h in range(2):
                cols = slice(h * 256 + part * 128, h * 256 + (part + 1) * 128)
                INB[:, cols] = message[:, h * 128:(h + 1) * 128]
        result(INB, inbox_out.at[0])

    AYzp, AYzq = first_hop("ZYp", "ZYm", rows_b, own), first_hop("ZYp", "ZYm", rows_b, rest)
    AYop, AYoq = first_hop("YZop", "YZom", rows_a, own), first_hop("YZop", "YZom", rows_a, rest)
    AYnp, AYnq = to_mate("ZYy0", rows_b, own), to_mate("ZYy0", rows_b, rest)
    AZay, AZby = pass_on("ZYym", mate, zm, yl, rows_b), pass_on("ZYyp", mate, zp, yl, rows_b)
    AZd = pass_on("YZfp", up_z, zm, yl, rows_a, "YZop")
    AZg = pass_on("YZfm", down_z, zp, my, rows_a, "YZmm")
    FS0, FS1 = pass_on("S0", sibling, z, yl, half(c)), pass_on("S1", sibling, z, my, rows_a)
    FSa, FSb = pass_on("Sa", sibling, zm, yl, rows_b), pass_on("Sb", sibling, zp, yl, rows_b)
    FSc, FSd = pass_on("Sc", sibling, z2, yl, rows_b), pass_on("Sd", sibling, zm, yl, rows_a)
    FSe, FSf = pass_on("Se", sibling, zp, yl, rows_a, "YZom"), pass_on("Sf", sibling, zm, my, rows_a, "YZmp")
    FSg, FSh = pass_on("Sg", sibling, zp, my, rows_a), pass_on("Sh", sibling, z2, yl, rows_a, "YZfp")
    FSi, FSya = pass_on("Si", sibling, z2, my, rows_a, "YZfm"), pass_on("Sya", sibling, z0, my, rows_b, "ZYy0")
    FSyb, FSyc = pass_on("Syb", sibling, zm, my, rows_b, "ZYym"), pass_on("Syc", sibling, zp, my, rows_b, "ZYyp")
    FSyd = pass_on("Syd", sibling, z2, my, rows_b, "ZYy2")

    barrier = pltpu.get_barrier_semaphore()
    others = [(lax.rem(rep + j, 4), fs) for j in (1, 2, 3)] + [mate, up_z, down_z]
    others += [at(core, z, x + j, yl) for core in (0, 1) for j in (1, 2, 3)]
    for other in others:
        pl.semaphore_signal(barrier, inc=1, device_id=other, device_id_type=MESH)
    for copy in numbers_in:
        copy.wait()
    WT[...] = jnp.where(lax.broadcasted_iota(jnp.int32, (8, 128), 0) < 4, weight[0], inbox_wt[0])
    for s in range(2):
        step = jnp.full((8, 128), index[s]).astype(F32)
        RATE[s] = 0.5 * math.sqrt(D / (TOK * 32)) * INV_ROOT * (1.0 + 0.5 * jnp.cos(jnp.pi * step / 1024.0))
    inputs[0].wait()
    project(0)
    inputs[1].wait()
    for s in range(2):
        UPL[s] = jnp.where(valid(s), COT[s].astype(F32), 0.0).astype(BF)
    inputs[2].wait()
    pl.semaphore_wait(barrier, len(others))

    send(("WT", 0), WT, WR.at[0], next1)
    send(("WT", 1), WT, WR.at[1], next2)
    for task, *numbers in (
        (AX, 0), (UPs, 0), (AYp, 0), (T, 0, 0), (AYop, 0), (AYzp, 0), (AY1p, 0), (AYq, 0), (AYzq, 0), (T, 0, 1),
        (AYoq, 0), (T, 0, 2), (UT, 0), (T, 0, 3), (AZa, 0), (AYnp, 0), (AY1, 0), (C, 0, 0), (AYnq, 0), (T, 0, 4),
        (C, 0, 1), (AZb, 0), (AZay, 0), (Dd, 0, 0), (AHm, 0), (AZby, 0), (Dd, 0, 1), (T, 0, 5), (AHp, 0), (FSa, 0),
        (T, 0, 6), (C, 0, 2), (Ee, 0, 0), (AZg, 0), (T, 0, 7), (C, 0, 3), (UPs, 1), (AZd, 0), (Dd, 0, 2), (C, 0, 4),
        (FSf, 0), (FS1, 0), (AZc, 0), (T, 1, 0), (C, 0, 5), (T, 1, 1), (Ee, 0, 2), (Ee, 0, 1), (FSg, 0), (T, 1, 2),
        (Dd, 0, 3), (Dd, 0, 4), (Fpl, 0), (Fml, 0), (Dd, 0, 5), (T, 1, 3), (C, 0, 6), (C, 0, 7), (Dd, 0, 6),
        (Ee, 0, 4), (Fph, 0), (FSyb, 0), (FSyc, 0), (Fmh, 0), (Gpl, 0), (Dd, 0, 7), (FSb, 0), (UT, 1), (C, 1, 0),
        (Hl, 0), (Ee, 0, 3), (Ee, 0, 5), (Gph, 0), (T, 1, 4), (Gmh, 0), (FSya, 0), (C, 1, 1), (FSh, 0), (Dd, 1, 0),
        (FSe, 0), (Gml, 0), (Hh, 0), (AHm, 1), (Dd, 1, 1), (AHp, 1), (C, 1, 2), (C, 1, 3), (T, 1, 5), (Dd, 1, 2),
        (Ee, 0, 6), (FSc, 0), (Fpl, 1), (Ee, 0, 7), (Ih, 0), (Ee, 1, 0), (C, 1, 4), (Dd, 1, 3), (FSd, 0),
        (Ee, 1, 1), (Fml, 1), (Il, 0), (Jl, 0), (Jh, 0), (Dd, 1, 4), (C, 1, 5), (T, 1, 6), (FS0, 0), (Fph, 1),
        (Ee, 1, 3), (UA, 0), (MSA, 0), (Gml, 1), (UB, 0), (Dd, 1, 5), (Fmh, 1), (AX, 1), (Ee, 1, 4), (Ee, 1, 2),
        (Gph, 1), (AYp, 1), (AYzp, 1), (AYop, 1), (MSB, 0), (T, 1, 7), (FSi, 0), (Gpl, 1), (AY1p, 1), (AYq, 1),
        (AYzq, 1), (C, 1, 6), (Ee, 1, 5), (FS0, 1), (AYoq, 1), (AYnq, 1), (FSyd, 0), (AYnp, 1), (V, 0, 2),
        (C, 1, 7), (Dd, 1, 6), (Dd, 1, 7), (AY1, 1), (Gmh, 1), (FSya, 1), (V, 0, 3), (AZa, 1), (Hh, 1), (AZb, 1),
        (AZby, 1), (V, 0, 1), (AZd, 1), (FSb, 1), (V, 0, 0), (VRet, 0), (FSe, 1), (FS1, 1), (AZg, 1), (Ee, 1, 7),
        (Hl, 1), (Ee, 1, 6), (AZay, 1), (Jh, 1), (FSg, 1), (Jl, 1), (FSyc, 1), (FSf, 1), (AZc, 1), (Ih, 1),
        (V, 1, 3), (FSa, 1), (Il, 1), (V, 1, 1), (FSc, 1), (FSd, 1), (FSyb, 1), (VM, 0), (UB, 1), (MSB, 1),
        (FSh, 1), (FSi, 1), (UA, 1), (FSyd, 1), (V, 1, 2), (MSA, 1), (V, 1, 0), (VRet, 1), (VM, 1), (M, 0),
    ):
        task(*numbers)
    for name in list(pending):
        sent(name)
    for copy in outputs:
        copy.wait()


def finish(val, num_out, inbox_out, w_out, mw_out, val_to, num_to, inbox_to, w_to, mw_to, VAL, NUM, INB, W, MW, sem):
    trips = [(num_out, NUM, num_to), (inbox_out, INB, inbox_to), (val, VAL, val_to), (w_out, W, w_to), (mw_out, MW, mw_to)]
    loads = [pltpu.make_async_copy(src, stop, sem.at[i]) for i, (src, stop, dst) in enumerate(trips)]
    stores = [pltpu.make_async_copy(stop, dst, sem.at[5 + i]) for i, (src, stop, dst) in enumerate(trips)]
    for copy in loads:
        copy.start()
    for load, store in zip(loads, stores):
        load.wait()
        store.start()
    for copy in stores:
        copy.wait()


def per_device(activations, cotangent, numerator, weight, inbox_num, inbox_wt, lengths, step_index):
    hbm = pl.BlockSpec(memory_space=pl.ANY)
    hb = 256 - HA
    matrix = jax.ShapeDtypeStruct((1, 256, HV), F32)
    scalar = jax.ShapeDtypeStruct((1,), F32)
    tokens = jax.ShapeDtypeStruct((2, 1, TOK, HV), BF)
    values, num_out, w_out, inbox_out, mw_out = pl.pallas_call(
        kernel,
        out_shape=(tokens, matrix, scalar, matrix, scalar),
        in_specs=[hbm] * 8,
        out_specs=(hbm,) * 5,
        scratch_shapes=[
            pltpu.VMEM((2, TOK, D), BF),
            pltpu.VMEM((2, 4, 4, 2, 256, HV), BF),
            pltpu.VMEM((4, 4, 2, 256, 256), BF),
            pltpu.VMEM((4, 4, 2, 256, 256), BF),
            pltpu.VMEM((4, 4, 2, 256, 256), BF),
            pltpu.VMEM((2, 2, 2, 2, HA, 256), BF),
            pltpu.VMEM((2, 2, 4, 2, HA, 256), BF),
            pltpu.VMEM((2, 4, HA, 256), BF),
            pltpu.VMEM((2, 4, 4, hb, 256), BF),
            pltpu.VMEM((2, 2, 2, hb, 256), BF),
            pltpu.VMEM((2, 2, 4, hb, 256), BF),
            pltpu.VMEM((2, 2, 2, 256, 256), BF),
            pltpu.VMEM((2, TOK, HV), BF),
            pltpu.VMEM((2, TOK, HV), BF),
            pltpu.VMEM((2, HV, TOK), BF),
            pltpu.VMEM((2, TOK, HV), BF),
            pltpu.VMEM((2, TOK, HV), BF),
            pltpu.VMEM((TOK, HV), F32),
            pltpu.VMEM((2, 256, HV), BF),
            pltpu.VMEM((2, 2, 256, 256), BF),
            pltpu.VMEM((2, 2, 2, 256, 256), BF),
            pltpu.VMEM((256, HV), F32),
            pltpu.VMEM((8, 128), F32),
            pltpu.VMEM((2, 8, 128), F32),
            pltpu.VMEM((2, TOK, HV), BF),
            pltpu.VMEM((256, HV), F32),
            pltpu.VMEM((256, HV), F32),
            pltpu.VMEM((2, 8, 128), F32),
            pltpu.SMEM((2,), jnp.int32),
            pltpu.SMEM((2,), jnp.int32),
            pltpu.SMEM((1,), F32),
            pltpu.SMEM((1,), F32),
            pltpu.SMEM((1,), F32),
            pltpu.SMEM((1,), F32),
            pltpu.SemaphoreType.DMA((320,)),
            pltpu.SemaphoreType.DMA((320,)),
            pltpu.SemaphoreType.DMA((16,)),
            pltpu.SemaphoreType.REGULAR((8,)),
        ],
        compiler_params=pltpu.CompilerParams(
            collective_id=0, has_side_effects=True, vmem_limit_bytes=63 * 2**20
        ),
        cost_estimate=pl.CostEstimate(flops=4 * 2 * TOK * D * HV, bytes_accessed=2 * TOK * D * 2, transcendentals=0),
        name="push_steps",
    )(step_index, lengths[:, 0, 0], weight, inbox_wt, activations, cotangent, numerator, inbox_num)
    values, num_out, inbox_out, w_out, mw_out = pl.pallas_call(
        finish,
        out_shape=(tokens, matrix, matrix, scalar, scalar),
        in_specs=[hbm] * 5,
        out_specs=(hbm,) * 5,
        scratch_shapes=[
            pltpu.VMEM((2, 1, TOK, HV), BF),
            pltpu.VMEM((1, 256, HV), F32),
            pltpu.VMEM((1, 256, HV), F32),
            pltpu.SMEM((1,), F32),
            pltpu.SMEM((1,), F32),
            pltpu.SemaphoreType.DMA((10,)),
        ],
        name="finish",
    )(values, num_out, inbox_out, w_out, mw_out)
    return values, num_out, w_out, inbox_out, mw_out


def solution(mesh):
    in_specs = (
        P(None, "rep", "fsdp", None),
        P(None, "rep", "fsdp", None),
        P("rep", "fsdp", None),
        P("rep"),
        P("rep", "fsdp", None),
        P("rep"),
        P(None, "rep", "fsdp"),
        P(),
    )
    out_specs = (
        P(None, "rep", "fsdp", None),
        P("rep", "fsdp", None),
        P("rep"),
        P("rep", "fsdp", None),
        P("rep"),
    )
    return jax.shard_map(
        per_device, mesh=mesh, in_specs=in_specs, out_specs=out_specs, check_vma=False
    )
```

```python
import functools
import math

import jax
import jax.numpy as jnp
from jax import lax
from jax.experimental import pallas as pl
from jax.experimental.pallas import tpu as pltpu
from jax.sharding import PartitionSpec as P

MESH = pl.DeviceIdType.MESH
BF, F32 = jnp.bfloat16, jnp.float32
D, HV, TOK = 8192, 512, 384
INV_ROOT = 1.0 / math.sqrt(D)
HALF_TOK = TOK // 2
ROUTE = 96
HA = 128


def kernel(index_at, length_at, weight_at_, inbox_wt_at, act, cot, num, inbox, val, num_out, w_out, inbox_out, mw_out,
           ACT, Z, PT, PS, RSIB, RAH, RAF, RAY, RBY, RBH, RBF, RX, UPL, UP, UPT, VB, VR, VACC,
           ZS, KB, MSG, X1, WT, WR, COT, NUM, INB, RATE, index, length, weight, inbox_wt, wts0, wts1, ss, rs, io, credit):
    rep, fs = lax.axis_index("rep"), lax.axis_index("fsdp")
    yh, c = rep // 2, rep % 2
    z, x, yl = fs // 8, (fs // 2) % 4, fs % 2
    q = x % 2
    home = c == q
    guest = c != q
    my = 1 - yl

    def at(core, zz, xx, yy):
        return (yh * 2 + core, lax.rem(zz + 4, 4) * 8 + lax.rem(xx + 4, 4) * 2 + yy)

    sibling, mate = at(1 - c, z, x, yl), at(c, z, x, my)
    up_z, down_z = at(c, z + 1, x, yl), at(c, z + 3, x, yl)
    z0, zp, zm, z2 = z, lax.rem(z + 1, 4), lax.rem(z + 3, 4), lax.rem(z + 2, 4)
    chunk = (z2, zp, zm, z0)
    parts = ((z2, 0), (z2, 1), (zp, 0), (zm, 0), (zp, 1), (zm, 1), (z0, 0), (z0, 1))
    next1, next2 = (lax.rem(rep + 1, 4), fs), (lax.rem(rep + 2, 4), fs)

    inputs = [pltpu.make_async_copy(*pair, io.at[i])
              for i, pair in enumerate([(num.at[0], NUM), (cot.at[:, 0], COT), (inbox.at[0], INB)])]
    numbers_in = [pltpu.make_async_copy(*pair, io.at[3 + i]) for i, pair in enumerate(
        [(index_at, index), (length_at, length), (weight_at_, weight), (inbox_wt_at, inbox_wt)])]
    for copy in numbers_in + inputs:
        copy.start()
    names, pending = {}, {}

    def number(name):
        return names.setdefault(name, len(names))

    def remote(name, src, dst, to):
        k = number(name)
        r = number((name[0],) + name[2:]) if name[0].startswith("*") else k
        return pltpu.make_async_remote_copy(src, dst, ss.at[k], rs.at[r], device_id=to, device_id_type=MESH)

    def send(name, src, dst, to, guard=None):
        copy = remote(name, src, dst, to)
        pending[name] = (copy, guard)
        if guard is None:
            copy.start()
        else:
            pl.when(guard)(copy.start)

    def local(name, src, dst, guard):
        r = number((name[0],) + name[2:])
        pl.when(guard)(pltpu.make_async_copy(src, dst, rs.at[r]).start)

    def arrived(name, dst):
        r = number(name)
        pltpu.make_async_copy(dst, dst, rs.at[r]).wait()

    def sent(name):
        copy, guard = pending.pop(name)
        if guard is None:
            copy.wait_send()
        else:
            pl.when(guard)(copy.wait_send)

    def half(h):
        return pl.ds(pl.multiple_of(h * 128, 128), 128)

    rows_a = pl.ds(pl.multiple_of(c * 128, 64), ROUTE)
    rows_b = pl.ds(pl.multiple_of(c * 128 + ROUTE, 16), 128 - ROUTE)
    sib_a = pl.ds(pl.multiple_of((1 - c) * 128, 64), ROUTE)
    sib_b = pl.ds(pl.multiple_of((1 - c) * 128 + ROUTE, 16), 128 - ROUTE)
    hv_a, hv_b = pl.ds(0, HA), pl.ds(HA, 256 - HA)
    low, high, every = pl.ds(0, 2), pl.ds(2, 2), pl.ds(0, 4)
    pairs = (low, high)
    own, rest = pl.ds(0, 1), pl.ds(1, 3)

    def weight_at(s):
        return weight[0] if s == 0 else 0.5 * weight[0] + inbox_wt[0]

    def project(s):
        block = NUM[...] if s == 0 else X1[...]
        ZS[s] = (block / weight_at(s)).astype(BF)

    def AX(s):
        if s == 1:
            project(s)

        def shard(h, place):
            return ZS.at[s, half(h)], Z.at[s, z, place, yl, half(h)]

        send(("*AXo", 0, s), *shard(1 - c, 0), sibling, home)
        local(("*AXo", 1, s), *shard(c, 0), home)
        far, place = jnp.where(home, x + 2, x + 1), jnp.where(home, 2, 3)
        send(("*AX", 0, s), *shard(0, place), at(0, z, far, yl))
        send(("*AX", 1, s), *shard(1, place), at(1, z, far, yl))
        send(("*AX", 2, s), *shard(0, 1), at(0, z, x + 3, yl), guest)
        send(("*AX", 3, s), *shard(1, 1), at(1, z, x + 3, yl), guest)

    def gathered(s, zz, yy, rows, part=every):
        return Z.at[s, zz, part, yy, rows]

    def pass_on(name, to, zz, yy, rows, source=None, part=every):
        def run(s):
            piece = gathered(s, zz, yy, rows, part)
            if source in ("YZop", "YZom", "YZmp", "YZmm", "ZYy0"):
                both(source, s, zz, yy, rows)
            elif source is not None:
                arrived((source, s), piece)
            send((name, s), piece, piece, to)
        return run

    def both(name, s, zz, yy, rows):
        arrived((name, 0, s), gathered(s, zz, yy, rows, own))
        arrived((name, 1, s), gathered(s, zz, yy, rows, rest))

    def first_hop(plus, minus, rows, part, yy=yl):
        def run(s):
            piece = gathered(s, z, yy, rows, part)
            send((plus, int(part is rest), s), piece, piece, up_z)
            send((minus, int(part is rest), s), piece, piece, down_z)
        return run

    def to_mate(name, rows, part):
        def run(s):
            piece = gathered(s, z, yl, rows, part)
            send((name, int(part is rest), s), piece, piece, mate)
        return run

    def AYp(s):
        arrived(("*AXo", s), gathered(s, z, yl, half(c), own))
        to_mate("YZy", rows_a, own)(s)

    def AYq(s):
        arrived(("*AX", s), gathered(s, z, yl, half(c), rest))
        to_mate("YZy", rows_a, rest)(s)

    def AY1p(s):
        arrived(("YZy", 0, s), gathered(s, z, my, rows_a, own))
        first_hop("YZmp", "YZmm", rows_a, own, my)(s)

    def AY1(s):
        arrived(("YZy", 1, s), gathered(s, z, my, rows_a, rest))
        first_hop("YZmp", "YZmm", rows_a, rest, my)(s)

    def AZa(s):
        both("ZYp", s, zm, yl, rows_b)
        pass_on("ZYfp", up_z, zm, yl, rows_b, None, low)(s)

    def AZb(s):
        both("ZYm", s, zp, yl, rows_b)
        pass_on("ZYfm", down_z, zp, yl, rows_b, None, high)(s)

    def AZc(s):
        arrived(("ZYfp", s), gathered(s, z2, yl, rows_b, low))
        arrived(("ZYfm", s), gathered(s, z2, yl, rows_b, high))
        pass_on("ZYy2", mate, z2, yl, rows_b)(s)

    begun = set()

    def V(s, k):
        zz = chunk[k]
        if s not in begun:
            begun.add(s)
            VACC[...] = jnp.zeros_like(VACC)
        if k == 3:
            arrived(("S0", s), Z.at[s, z, :, yl, half(1 - c)])
            arrived(("S1", s), Z.at[s, z, :, my, sib_a])
            arrived(("Sya", s), Z.at[s, z, :, my, sib_b])
        else:
            four = {2: ("Sa", "Sd", "Sf", "Syb"), 1: ("Sb", "Se", "Sg", "Syc"), 0: ("Sc", "Sh", "Si", "Syd")}[k]
            for name, yy, piece in zip(four, (yl, yl, my, my), (sib_b, sib_a, sib_a, sib_b)):
                arrived((name, s), Z.at[s, zz, :, yy, piece])

        def body(j, carry):
            columns = pl.ds(pl.multiple_of(zz * 2048 + lax.rem(x + j, 4) * 512, 512), 512)
            VACC[...] += jnp.dot(ACT[s, :, columns], Z[s, zz, j].reshape(512, HV), preferred_element_type=F32)
            return carry

        lax.fori_loop(0, 4, body, 0)

    def VRet(s):
        VB[s] = (VACC[...] * INV_ROOT).astype(BF)
        top, low_rows = pl.ds(0, HALF_TOK), pl.ds(HALF_TOK, HALF_TOK)
        send(("*VR", 0, s), VB.at[s, top], VR.at[s, top], at(1 - c, z, x + 3, yl), guest)
        send(("*VR", 1, s), VB.at[s, low_rows], VR.at[s, low_rows], at(1 - c, z, x + 1, yl), guest)
        local(("*VR", 2, s), VB.at[s], VR.at[s], home)

    def valid(s):
        return lax.broadcasted_iota(jnp.int32, (TOK, HV), 0) < length[s]

    def VM(s):
        arrived(("*VR", s), VR.at[s])
        VR[s] = jnp.where(valid(s), VR[s].astype(F32), 0.0).astype(BF)
        result(VR.at[s], val.at[s, 0])

    outputs = []

    def result(src, dst):
        outputs.append(pltpu.make_async_copy(src, dst, io.at[7 + len(outputs)]))
        outputs[-1].start()

    def UPs(s):
        top, low_rows = pl.ds(0, HALF_TOK), pl.ds(HALF_TOK, HALF_TOK)
        send(("*UP", 0, s), UPL.at[s, top], UP.at[s, top], at(1 - c, z, x + 1, yl), guest)
        send(("*UP", 1, s), UPL.at[s, low_rows], UP.at[s, low_rows], at(1 - c, z, x + 3, yl), guest)
        local(("*UP", 2, s), UPL.at[s], UP.at[s], home)

    def UT(s):
        arrived(("*UP", s), UP.at[s])
        mine = UP[s, :, pl.ds(pl.multiple_of(c * 256, 256), 256)]
        UPT[s, 0:256] = mine.astype(F32).T.astype(BF)
        other = UP[s, :, pl.ds(pl.multiple_of((1 - c) * 256, 256), 256)]
        UPT[s, 256:512] = other.astype(F32).T.astype(BF)

    def columns_of(zz, xx):
        return pl.ds(pl.multiple_of(zz * 2048 + lax.rem(xx, 4) * 512, 512), 512)

    def T(s, k):
        zz, h = parts[k]
        for e in (2 * h, 2 * h + 1):
            for j, to in ((0, x + 1), (1, x + 3)):
                rows, cols = pl.ds(j * HALF_TOK, HALF_TOK), columns_of(zz, to + e)
                send(("*T", 4 * j + e, s, k), act.at[s, 0, rows, cols], ACT.at[s, rows, cols],
                     at(1 - c, z, to, yl), guest)
            cols = columns_of(zz, x + e)
            local(("*T", 8 + e, s, k), act.at[s, 0, :, cols], ACT.at[s, :, cols], home)

    def C(s, k):
        zz, h = parts[k]
        arrived(("*T", s, k), ACT.at[s, :, pl.ds(0, 1024)])
        if s == 1:
            used = (("Ahm", "Bhm"), ("Ahp", "Bhp"), ("Afpl", "Bfpl"), ("Afml", "Bfml"), ("Afph", "Bfph"),
                    ("Afmh", "Bfmh"), ("Ayl",), ("Ayh",))[k]
            for name in used:
                sent((name, 0))
            sent(("By", 0, k))
            sent(("SIB", 0, k))
            if k >= 6:
                for part in range(2):
                    for j in (2 * h, 2 * h + 1):
                        sent(("*X", j, part, 0))
            pl.semaphore_wait(credit.at[k], 1)

        def body(j, carry):
            block = jnp.dot(UPT[s], ACT[s, :, columns_of(zz, x + j)], preferred_element_type=F32).astype(BF)
            for yy in range(2):
                PT[zz, j, yy] = block[0:256, yy * 256:(yy + 1) * 256]
                PS[zz, j, yy] = block[256:512, yy * 256:(yy + 1) * 256]
            return carry

        lax.fori_loop(2 * h, 2 * h + 2, body, 0)
        send(("SIB", s, k), PS.at[zz, pairs[h]], RSIB.at[zz, pairs[h]], sibling)

    def add_into(count, target, *others):
        def body(j, carry):
            total = target(j)[...].astype(F32)
            for other in others:
                total = total + other(j)[...].astype(F32)
            target(j)[...] = total.astype(BF)
            return carry
        lax.fori_loop(0, count, body, 0)

    def Dd(s, k):
        zz, h = parts[k]
        arrived(("SIB", s, k), RSIB.at[zz, pairs[h]])
        add_into(4, lambda j: PT.at[zz, 2 * h + j // 2, j % 2], lambda j: RSIB.at[zz, 2 * h + j // 2, j % 2])
        if s == 0:
            pl.semaphore_signal(credit.at[k], inc=1, device_id=sibling, device_id_type=MESH)
        send(("By", s, k), PT.at[zz, pairs[h], my, hv_b], RBY.at[s, zz, pairs[h]], mate)

    def Ee(s, k):
        zz, h = parts[k]
        arrived(("By", s, k), RBY.at[s, zz, pairs[h]])
        add_into(2, lambda j: PT.at[zz, 2 * h + j, yl, hv_b], lambda j: RBY.at[s, zz, 2 * h + j])
        if k == 0:
            send(("Bhm", s), PT.at[zz, low, yl, hv_b], RBH.at[s, 0], down_z)
        if k == 1:
            send(("Bhp", s), PT.at[zz, high, yl, hv_b], RBH.at[s, 1], up_z)

    def AHm(s):
        send(("Ahm", s), PT.at[z2, low, :, hv_a], RAH.at[s, 0], down_z)

    def AHp(s):
        send(("Ahp", s), PT.at[z2, high, :, hv_a], RAH.at[s, 1], up_z)

    def Fml(s):
        arrived(("Ahm", s), RAH.at[s, 0])
        add_into(4, lambda j: PT.at[zm, j // 2, j % 2, hv_a], lambda j: RAH.at[s, 0, j // 2, j % 2])
        send(("Afml", s), PT.at[zm, low, :, hv_a], RAF.at[s, 0, low], down_z)

    def Fmh(s):
        send(("Afmh", s), PT.at[zm, high, :, hv_a], RAF.at[s, 0, high], down_z)

    def Fpl(s):
        send(("Afpl", s), PT.at[zp, low, :, hv_a], RAF.at[s, 1, low], up_z)

    def Fph(s):
        arrived(("Ahp", s), RAH.at[s, 1])
        add_into(4, lambda j: PT.at[zp, 2 + j // 2, j % 2, hv_a], lambda j: RAH.at[s, 1, j // 2, j % 2])
        send(("Afph", s), PT.at[zp, high, :, hv_a], RAF.at[s, 1, high], up_z)

    def Gmh(s):
        send(("Bfmh", s), PT.at[zm, high, yl, hv_b], RBF.at[s, 0, high], down_z)

    def Gml(s):
        arrived(("Bhm", s), RBH.at[s, 0])
        add_into(2, lambda j: PT.at[zm, j, yl, hv_b], lambda j: RBH.at[s, 0, j])
        send(("Bfml", s), PT.at[zm, low, yl, hv_b], RBF.at[s, 0, low], down_z)

    def Gpl(s):
        send(("Bfpl", s), PT.at[zp, low, yl, hv_b], RBF.at[s, 1, low], up_z)

    def Gph(s):
        arrived(("Bhp", s), RBH.at[s, 1])
        add_into(2, lambda j: PT.at[zp, 2 + j, yl, hv_b], lambda j: RBH.at[s, 1, j])
        send(("Bfph", s), PT.at[zp, high, yl, hv_b], RBF.at[s, 1, high], up_z)

    def H(s, h, minus, plus, name):
        arrived((minus, s), RAF.at[s, 0, pairs[h]])
        arrived((plus, s), RAF.at[s, 1, pairs[h]])
        add_into(4, lambda j: PT.at[z, 2 * h + j // 2, j % 2, hv_a], lambda j: RAF.at[s, 0, 2 * h + j // 2, j % 2],
                 lambda j: RAF.at[s, 1, 2 * h + j // 2, j % 2])
        send((name, s), PT.at[z, pairs[h], my, hv_a], RAY.at[s, pairs[h]], mate)

    def Hl(s):
        H(s, 0, "Afml", "Afpl", "Ayl")

    def Hh(s):
        H(s, 1, "Afmh", "Afph", "Ayh")

    def owners(s, part, hv, h):
        def piece(place, i):
            return PT.at[z, place, yl, hv], RX.at[s, i, c, hv]

        if h == 0:
            send(("*X", 1, part, s), *piece(1, 1), at(q, z, x + 1, yl))
            send(("*X", 0, part, s), *piece(0, 0), sibling, guest)
            local(("*X", 4, part, s), *piece(0, 0), home)
        else:
            send(("*X", 2, part, s), *piece(2, 1), at(q, z, x + 2, yl))
            send(("*X", 3, part, s), *piece(3, 0), at(q, z, x + 3, yl))

    def I(s, h, name):
        arrived((name, s), RAY.at[s, pairs[h]])
        add_into(2, lambda j: PT.at[z, 2 * h + j, yl, hv_a], lambda j: RAY.at[s, 2 * h + j])
        owners(s, 0, hv_a, h)

    def Il(s):
        I(s, 0, "Ayl")

    def Ih(s):
        I(s, 1, "Ayh")

    def J(s, h, minus, plus):
        arrived((minus, s), RBF.at[s, 0, pairs[h]])
        arrived((plus, s), RBF.at[s, 1, pairs[h]])
        add_into(2, lambda j: PT.at[z, 2 * h + j, yl, hv_b], lambda j: RBF.at[s, 0, 2 * h + j],
                 lambda j: RBF.at[s, 1, 2 * h + j])
        owners(s, 1, hv_b, h)

    def Jl(s):
        J(s, 0, "Bfml", "Bfpl")

    def Jh(s):
        J(s, 1, "Bfmh", "Bfph")

    def chosen(s, part):
        return jnp.where(jnp.full((256, 256), index[s] % 2) == 0, MSG[s, 0, part].astype(F32),
                         MSG[s, 1, part].astype(F32))

    def U(s, part, hv):
        arrived(("*X", part, s), RX.at[s, :, :, hv])
        if s == 1:
            for j in range(2):
                arrived(("MSG", j, part, 0), MSG.at[0, j, part])
            message = chosen(0, part)
        for h in range(2):
            mine, cols = slice(h * 128, (h + 1) * 128), slice(h * 256 + part * 128, h * 256 + (part + 1) * 128)
            grad = (RX[s, 0, h, hv].astype(F32) + RX[s, 1, h, hv].astype(F32)).T
            block = NUM[:, cols] if s == 0 else X1[:, cols]
            kept = 0.5 * (block - RATE[s, 0:1, 0:1] * grad)
            KB[s, part, :, mine] = kept.astype(BF)
            X1[:, cols] = kept + (INB[:, cols] if s == 0 else message[:, mine])

    def weights():
        for j in range(2):
            arrived(("WT", j), WR.at[j])
        even0, even1 = index[0] % 2 == 0, index[1] % 2 == 0
        wts0[0] = 0.5 * weight_at(1) + 0.5 * jnp.where(even0, WR[0, 0, 0], WR[1, 0, 0])
        wts1[0] = 0.5 * (0.5 * jnp.where(even1, WR[0, 0, 0], WR[1, 0, 0])
                           + jnp.where(even1, WR[0, 4, 0], WR[1, 4, 0]))
        result(wts0, w_out)
        result(wts1, mw_out)

    def UA(s):
        U(s, 0, hv_a)
        if s == 0:
            weights()

    def UB(s):
        U(s, 1, hv_b)

    def MS(s, part):
        send(("MSG", 0, part, s), KB.at[s, part], MSG.at[s, 0, part], next1)
        send(("MSG", 1, part, s), KB.at[s, part], MSG.at[s, 1, part], next2)

    def MSA(s):
        MS(s, 0)

    def MSB(s):
        MS(s, 1)

    def M(s):
        result(X1, num_out.at[0])
        for part in range(2):
            for j in range(2):
                arrived(("MSG", j, part, 1), MSG.at[1, j, part])
            message = chosen(1, part)
            for h in range(2):
                cols = slice(h * 256 + part * 128, h * 256 + (part + 1) * 128)
                INB[:, cols] = message[:, h * 128:(h + 1) * 128]
        result(INB, inbox_out.at[0])

    AYzp, AYzq = first_hop("ZYp", "ZYm", rows_b, own), first_hop("ZYp", "ZYm", rows_b, rest)
    AYop, AYoq = first_hop("YZop", "YZom", rows_a, own), first_hop("YZop", "YZom", rows_a, rest)
    AYnp, AYnq = to_mate("ZYy0", rows_b, own), to_mate("ZYy0", rows_b, rest)
    AZay, AZby = pass_on("ZYym", mate, zm, yl, rows_b), pass_on("ZYyp", mate, zp, yl, rows_b)
    AZd = pass_on("YZfp", up_z, zm, yl, rows_a, "YZop")
    AZg = pass_on("YZfm", down_z, zp, my, rows_a, "YZmm")
    FS0, FS1 = pass_on("S0", sibling, z, yl, half(c)), pass_on("S1", sibling, z, my, rows_a)
    FSa, FSb = pass_on("Sa", sibling, zm, yl, rows_b), pass_on("Sb", sibling, zp, yl, rows_b)
    FSc, FSd = pass_on("Sc", sibling, z2, yl, rows_b), pass_on("Sd", sibling, zm, yl, rows_a)
    FSe, FSf = pass_on("Se", sibling, zp, yl, rows_a, "YZom"), pass_on("Sf", sibling, zm, my, rows_a, "YZmp")
    FSg, FSh = pass_on("Sg", sibling, zp, my, rows_a), pass_on("Sh", sibling, z2, yl, rows_a, "YZfp")
    FSi, FSya = pass_on("Si", sibling, z2, my, rows_a, "YZfm"), pass_on("Sya", sibling, z0, my, rows_b, "ZYy0")
    FSyb, FSyc = pass_on("Syb", sibling, zm, my, rows_b, "ZYym"), pass_on("Syc", sibling, zp, my, rows_b, "ZYyp")
    FSyd = pass_on("Syd", sibling, z2, my, rows_b, "ZYy2")

    barrier = pltpu.get_barrier_semaphore()
    others = [(lax.rem(rep + j, 4), fs) for j in (1, 2, 3)] + [mate, up_z, down_z]
    others += [at(core, z, x + j, yl) for core in (0, 1) for j in (1, 2, 3)]
    for other in others:
        pl.semaphore_signal(barrier, inc=1, device_id=other, device_id_type=MESH)
    for copy in numbers_in:
        copy.wait()
    WT[...] = jnp.where(lax.broadcasted_iota(jnp.int32, (8, 128), 0) < 4, weight[0], inbox_wt[0])
    for s in range(2):
        step = jnp.full((8, 128), index[s]).astype(F32)
        RATE[s] = 0.5 * math.sqrt(D / (TOK * 32)) * INV_ROOT * (1.0 + 0.5 * jnp.cos(jnp.pi * step / 1024.0))
    inputs[0].wait()
    project(0)
    inputs[1].wait()
    for s in range(2):
        UPL[s] = jnp.where(valid(s), COT[s].astype(F32), 0.0).astype(BF)
    inputs[2].wait()
    pl.semaphore_wait(barrier, len(others))

    send(("WT", 0), WT, WR.at[0], next1)
    send(("WT", 1), WT, WR.at[1], next2)
    for task, *numbers in (
        (AX, 0), (UPs, 0), (AYp, 0), (T, 0, 0), (AYop, 0), (AYzp, 0), (AY1p, 0), (AYq, 0), (AYzq, 0), (T, 0, 1),
        (AYoq, 0), (T, 0, 2), (UT, 0), (T, 0, 3), (AZa, 0), (AYnp, 0), (AY1, 0), (C, 0, 0), (AYnq, 0), (T, 0, 4),
        (C, 0, 1), (AZb, 0), (AZay, 0), (Dd, 0, 0), (AHm, 0), (AZby, 0), (Dd, 0, 1), (T, 0, 5), (AHp, 0), (FSa, 0),
        (T, 0, 6), (C, 0, 2), (Ee, 0, 0), (AZg, 0), (T, 0, 7), (C, 0, 3), (UPs, 1), (AZd, 0), (Dd, 0, 2), (C, 0, 4),
        (FSf, 0), (FS1, 0), (AZc, 0), (T, 1, 0), (C, 0, 5), (T, 1, 1), (Ee, 0, 2), (Ee, 0, 1), (FSg, 0), (T, 1, 2),
        (Dd, 0, 3), (Dd, 0, 4), (Fpl, 0), (Fml, 0), (Dd, 0, 5), (T, 1, 3), (C, 0, 6), (C, 0, 7), (Dd, 0, 6),
        (Ee, 0, 4), (Fph, 0), (FSyb, 0), (FSyc, 0), (Fmh, 0), (Gpl, 0), (Dd, 0, 7), (FSb, 0), (UT, 1), (C, 1, 0),
        (Hl, 0), (Ee, 0, 3), (Ee, 0, 5), (Gph, 0), (T, 1, 4), (Gmh, 0), (FSya, 0), (C, 1, 1), (FSh, 0), (Dd, 1, 0),
        (FSe, 0), (Gml, 0), (Hh, 0), (AHm, 1), (Dd, 1, 1), (AHp, 1), (C, 1, 2), (C, 1, 3), (T, 1, 5), (Dd, 1, 2),
        (Ee, 0, 6), (FSc, 0), (Fpl, 1), (Ee, 0, 7), (Ih, 0), (Ee, 1, 0), (C, 1, 4), (Dd, 1, 3), (FSd, 0),
        (Ee, 1, 1), (Fml, 1), (Il, 0), (Jl, 0), (Jh, 0), (Dd, 1, 4), (C, 1, 5), (T, 1, 6), (FS0, 0), (Fph, 1),
        (Ee, 1, 3), (UA, 0), (MSA, 0), (Gml, 1), (UB, 0), (Dd, 1, 5), (Fmh, 1), (AX, 1), (Ee, 1, 4), (Ee, 1, 2),
        (Gph, 1), (AYp, 1), (AYzp, 1), (AYop, 1), (MSB, 0), (T, 1, 7), (FSi, 0), (Gpl, 1), (AY1p, 1), (AYq, 1),
        (AYzq, 1), (C, 1, 6), (Ee, 1, 5), (FS0, 1), (AYoq, 1), (AYnq, 1), (FSyd, 0), (AYnp, 1), (V, 0, 2),
        (C, 1, 7), (Dd, 1, 6), (Dd, 1, 7), (AY1, 1), (Gmh, 1), (FSya, 1), (V, 0, 3), (AZa, 1), (Hh, 1), (AZb, 1),
        (AZby, 1), (V, 0, 1), (AZd, 1), (FSb, 1), (V, 0, 0), (VRet, 0), (FSe, 1), (FS1, 1), (AZg, 1), (Ee, 1, 7),
        (Hl, 1), (Ee, 1, 6), (AZay, 1), (Jh, 1), (FSg, 1), (Jl, 1), (FSyc, 1), (FSf, 1), (AZc, 1), (Ih, 1),
        (V, 1, 3), (FSa, 1), (Il, 1), (V, 1, 1), (FSc, 1), (FSd, 1), (FSyb, 1), (VM, 0), (UB, 1), (MSB, 1),
        (FSh, 1), (FSi, 1), (UA, 1), (FSyd, 1), (V, 1, 2), (MSA, 1), (V, 1, 0), (VRet, 1), (VM, 1), (M, 0),
    ):
        task(*numbers)
    for name in list(pending):
        sent(name)
    for copy in outputs:
        copy.wait()


def finish(val, num_out, inbox_out, w_out, mw_out, val_to, num_to, inbox_to, w_to, mw_to, VAL, NUM, INB, W, MW, sem):
    trips = [(val.at[s], VAL.at[s], val_to.at[s]) for s in range(2)]
    trips += [(num_out, NUM, num_to), (inbox_out, INB, inbox_to), (w_out, W, w_to), (mw_out, MW, mw_to)]
    loads = [pltpu.make_async_copy(src, stop, sem.at[i]) for i, (src, stop, dst) in enumerate(trips)]
    stores = [pltpu.make_async_copy(stop, dst, sem.at[6 + i]) for i, (src, stop, dst) in enumerate(trips)]
    for copy in loads:
        copy.start()
    for load, store in zip(loads, stores):
        load.wait()
        store.start()
    for copy in stores:
        copy.wait()


def per_device(activations, cotangent, numerator, weight, inbox_num, inbox_wt, lengths, step_index):
    hbm = pl.BlockSpec(memory_space=pl.ANY)
    hb = 256 - HA
    matrix = jax.ShapeDtypeStruct((1, 256, HV), F32)
    scalar = jax.ShapeDtypeStruct((1,), F32)
    tokens = jax.ShapeDtypeStruct((2, 1, TOK, HV), BF)
    values, num_out, w_out, inbox_out, mw_out = pl.pallas_call(
        kernel,
        out_shape=(tokens, matrix, scalar, matrix, scalar),
        in_specs=[hbm] * 8,
        out_specs=(hbm,) * 5,
        scratch_shapes=[
            pltpu.VMEM((2, TOK, D), BF),
            pltpu.VMEM((2, 4, 4, 2, 256, HV), BF),
            pltpu.VMEM((4, 4, 2, 256, 256), BF),
            pltpu.VMEM((4, 4, 2, 256, 256), BF),
            pltpu.VMEM((4, 4, 2, 256, 256), BF),
            pltpu.VMEM((2, 2, 2, 2, HA, 256), BF),
            pltpu.VMEM((2, 2, 4, 2, HA, 256), BF),
            pltpu.VMEM((2, 4, HA, 256), BF),
            pltpu.VMEM((2, 4, 4, hb, 256), BF),
            pltpu.VMEM((2, 2, 2, hb, 256), BF),
            pltpu.VMEM((2, 2, 4, hb, 256), BF),
            pltpu.VMEM((2, 2, 2, 256, 256), BF),
            pltpu.VMEM((2, TOK, HV), BF),
            pltpu.VMEM((2, TOK, HV), BF),
            pltpu.VMEM((2, HV, TOK), BF),
            pltpu.VMEM((2, TOK, HV), BF),
            pltpu.VMEM((2, TOK, HV), BF),
            pltpu.VMEM((TOK, HV), F32),
            pltpu.VMEM((2, 256, HV), BF),
            pltpu.VMEM((2, 2, 256, 256), BF),
            pltpu.VMEM((2, 2, 2, 256, 256), BF),
            pltpu.VMEM((256, HV), F32),
            pltpu.VMEM((8, 128), F32),
            pltpu.VMEM((2, 8, 128), F32),
            pltpu.VMEM((2, TOK, HV), BF),
            pltpu.VMEM((256, HV), F32),
            pltpu.VMEM((256, HV), F32),
            pltpu.VMEM((2, 8, 128), F32),
            pltpu.SMEM((2,), jnp.int32),
            pltpu.SMEM((2,), jnp.int32),
            pltpu.SMEM((1,), F32),
            pltpu.SMEM((1,), F32),
            pltpu.SMEM((1,), F32),
            pltpu.SMEM((1,), F32),
            pltpu.SemaphoreType.DMA((320,)),
            pltpu.SemaphoreType.DMA((320,)),
            pltpu.SemaphoreType.DMA((16,)),
            pltpu.SemaphoreType.REGULAR((8,)),
        ],
        compiler_params=pltpu.CompilerParams(
            collective_id=0, has_side_effects=True, vmem_limit_bytes=63 * 2**20
        ),
        cost_estimate=pl.CostEstimate(flops=4 * 2 * TOK * D * HV, bytes_accessed=2 * TOK * D * 2, transcendentals=0),
        name="push_steps",
    )(step_index, lengths[:, 0, 0], weight, inbox_wt, activations, cotangent, numerator, inbox_num)
    values, num_out, inbox_out, w_out, mw_out = pl.pallas_call(
        finish,
        out_shape=(tokens, matrix, matrix, scalar, scalar),
        in_specs=[hbm] * 5,
        out_specs=(hbm,) * 5,
        scratch_shapes=[
            pltpu.VMEM((2, 1, TOK, HV), BF),
            pltpu.VMEM((1, 256, HV), F32),
            pltpu.VMEM((1, 256, HV), F32),
            pltpu.SMEM((1,), F32),
            pltpu.SMEM((1,), F32),
            pltpu.SemaphoreType.DMA((12,)),
        ],
        name="finish",
    )(values, num_out, inbox_out, w_out, mw_out)
    return values, num_out, w_out, inbox_out, mw_out


def solution(mesh):
    in_specs = (
        P(None, "rep", "fsdp", None),
        P(None, "rep", "fsdp", None),
        P("rep", "fsdp", None),
        P("rep"),
        P("rep", "fsdp", None),
        P("rep"),
        P(None, "rep", "fsdp"),
        P(),
    )
    out_specs = (
        P(None, "rep", "fsdp", None),
        P("rep", "fsdp", None),
        P("rep"),
        P("rep", "fsdp", None),
        P("rep"),
    )
    return jax.shard_map(
        per_device, mesh=mesh, in_specs=in_specs, out_specs=out_specs, check_vma=False
    )
```
